256 devices in a mesh: dom: 64 (over z, y, core), feat: 4 (over x).
Axes of the slice: x: 4, y: 4, z: 8, core: 2. Of those that a mesh axis runs over, the one named last changes fastest.
Arguments:
- features: float32 [262144, 256], P('dom', 'feat'), may hold values from -6 to 6
- w_self: float32 [256, 256], P(None, 'feat'), may hold values from -0.375 to 0.375
- w_neigh: float32 [256, 256], P(None, 'feat'), may hold values from -0.375 to 0.375
- out_bias: float32 [256], P('feat'), may hold values from -3 to 3
- hub_rows: int32 [64, 64], P('dom'), may hold values from 0 to 4095
- replica_send_rows: int32 [64, 64, 128], P('dom'), may hold values from 0 to 4095
- ret_rows: int32 [64, 64, 64], P('dom'), may hold values from 0 to 4096, as said below
- tile_src: int32 [64, 96], P('dom'), may hold values from 0 to 95, each once within a row
- tile_dst: int32 [64, 96], P('dom'), may hold values from 0 to 31
- tile_vals: float32 [64, 96, 128, 128], P('dom'), may hold values from 0 to 0.086752765
Outputs:
- hidden_out: float32 [262144, 256], P('dom', 'feat')
The draws below stay inside these ranges and needn't reach their ends.
Inputs may be any that keep to these rules, and one draw needn't show every extreme that they name: `hub_rows`: rows of the partition that holds the list. replica_send_rows[q, p, s] is a row of partition q; lists may repeat rows. ret_rows[q, p, s] is a row of partition q, or 4096 for an empty slot; every block of 64 slots fills from the front with at least one row, and some blocks are full. `tile_src`: each partition's tiles use every source tile row once.
All inputs are finite; a program needn't handle non-finite values.
Results may differ from the reference program's by a relative error of at most 0.000065.
Values sent between devices are 32-bit elements; how exact they have to be, the bound alone decides.
No kernel may reach another device: no remote copies, remote signals or barrier semaphores. Data moves between devices by JAX's collectives and lax.ppermute only.
A program may use at most 64 MiB of HBM per device.

```python
import jax
import jax.numpy as jnp
from jax import lax

HIDDEN_WIDTH = 256
TB = 128
V_DEV = 4096
HUBS = 4096
MIRROR_ROW_COUNT = 8192
V = 262144
HUB_DEV = 64
SLOT = 128
RET = 64
TILES = 96
DST_BLOCKS = 32
N_DOM = 64


def draw_ret_rows(key, part):
    key = jax.random.fold_in(key, 7)
    key_count, key_rows = jax.random.split(key)
    counts = jax.random.randint(key_count, (N_DOM, N_DOM, 1), 1, RET + 1)
    master = jnp.arange(N_DOM)[:, None, None]
    mirror = jnp.arange(N_DOM)[None, :, None]
    counts = jnp.where(mirror == (master + 1) % N_DOM, RET, counts)
    counts = jnp.where(mirror == master, RET // 2, counts)
    rows = jax.random.randint(key_rows, (N_DOM, N_DOM, RET), 0, V_DEV)
    position = jnp.arange(RET)[None, None, :]
    return jnp.where(position < counts, rows, V_DEV).astype(jnp.int32)


def place_ends(values, own_key, least, largest):
    extent = values.shape
    spot = [jax.random.randint(jax.random.fold_in(own_key, axis), (), 0, extent[axis]) for axis in range(len(extent))]
    values = values.at[tuple(spot)].set(least)
    longest = extent.index(max(extent))
    spot[longest] = (spot[longest] + 1) % extent[longest]
    return values.at[tuple(spot)].set(largest)


def steps_of(own_key, extent, shards, smallest, largest):
    level = 1.0
    for dim, blocks in shards:
        steps = jax.random.uniform(jax.random.fold_in(jax.random.fold_in(own_key, 6), dim), (blocks,), jnp.float32, smallest / len(shards), largest / len(shards))
        level = level * jnp.repeat(jnp.exp(steps), extent[dim] // blocks).reshape((-1,) + (1,) * (len(extent) - 1 - dim))
    return level


def bell_draw(own_key, extent, deviation, limit, cuts=(), kind=jnp.bfloat16):
    result = deviation * jax.random.normal(own_key, extent, jnp.float32)
    if cuts:
        result = result * steps_of(own_key, extent, cuts, -0.22, 0.18)
    return jnp.clip(result, -limit, limit).astype(kind)


def setup_inputs(seed: int = 0) -> dict:
    arg_keys = jax.random.split(jax.random.key(seed), 11)
    return {
        "features": bell_draw(arg_keys[0], (V, HIDDEN_WIDTH), 1.0, 6.0, ((0, 64), (1, 4)), jnp.float32),
        "w_self": bell_draw(arg_keys[1], (HIDDEN_WIDTH, HIDDEN_WIDTH), HIDDEN_WIDTH ** -0.5, 0.375, ((1, 4),), jnp.float32),
        "w_neigh": bell_draw(arg_keys[2], (HIDDEN_WIDTH, HIDDEN_WIDTH), HIDDEN_WIDTH ** -0.5, 0.375, ((1, 4),), jnp.float32),
        "out_bias": bell_draw(arg_keys[3], (HIDDEN_WIDTH,), 0.5, 3.0, ((0, 4),), jnp.float32),
        "hub_rows": place_ends(jax.random.randint(arg_keys[4], (N_DOM, HUB_DEV), 0, V_DEV), jax.random.fold_in(arg_keys[4], 1), 0, V_DEV - 1).astype(jnp.int32),
        "replica_send_rows": place_ends(jax.random.randint(arg_keys[5], (N_DOM, N_DOM, SLOT), 0, V_DEV), jax.random.fold_in(arg_keys[5], 1), 0, V_DEV - 1).astype(jnp.int32),
        "ret_rows": draw_ret_rows(jax.random.fold_in(arg_keys[10], 71), 0),
        "tile_src": jax.vmap(lambda own: jax.random.permutation(own, TILES))(jax.random.split(arg_keys[7], N_DOM)).reshape((N_DOM, TILES)).astype(jnp.int32),
        "tile_dst": place_ends(jax.random.randint(arg_keys[8], (N_DOM, TILES), 0, DST_BLOCKS), jax.random.fold_in(arg_keys[8], 1), 0, DST_BLOCKS - 1).astype(jnp.int32),
        "tile_vals": jnp.clip(0.086752765 * jax.random.uniform(arg_keys[9], (N_DOM, TILES, TB, TB), jnp.float32) ** steps_of(arg_keys[9], (N_DOM, TILES, TB, TB), ((0, 64),), -0.2, 0.2), 0.0, 0.086752765),
    }


def project(left, right):
    return jnp.dot(left, right, precision=lax.Precision.HIGHEST, preferred_element_type=jnp.float32)


def reference(features, w_self, w_neigh, out_bias, hub_rows, replica_send_rows, ret_rows, tile_src, tile_dst, tile_vals):
    own_term = project(features, w_self)
    projected_rows = project(features, w_neigh).reshape(N_DOM, V_DEV, HIDDEN_WIDTH)
    owner_parts = jnp.arange(N_DOM, dtype=jnp.int32)
    hub_table = projected_rows[owner_parts[:, None], hub_rows].reshape(HUBS, HIDDEN_WIDTH)

    def mirror(row_index):
        received_rows = projected_rows[owner_parts[:, None], replica_send_rows[:, row_index, :]].reshape(MIRROR_ROW_COUNT, HIDDEN_WIDTH)
        whole = jnp.concatenate([hub_table, received_rows], axis=0).reshape(TILES, TB, HIDDEN_WIDTH)
        picked = whole[tile_src[row_index]]
        products = jnp.einsum("tij,tjf->tif", tile_vals[row_index], picked, precision=lax.Precision.HIGHEST, preferred_element_type=jnp.float32)
        buffer = jnp.zeros((DST_BLOCKS, TB, HIDDEN_WIDTH), jnp.float32).at[tile_dst[row_index]].add(products)
        return buffer.reshape(N_DOM, RET, HIDDEN_WIDTH)

    partial_sums = lax.map(mirror, owner_parts)
    arranged = jnp.transpose(partial_sums, (1, 0, 2, 3))
    summed = jnp.zeros((N_DOM, V_DEV, HIDDEN_WIDTH), jnp.float32).at[owner_parts[:, None, None], ret_rows].add(arranged, mode="drop")
    return jax.nn.relu(own_term + summed.reshape(N_DOM * V_DEV, HIDDEN_WIDTH) + out_bias)
```

```python
import functools

import jax
import jax.numpy as jnp
from jax import lax
from jax.experimental import pallas as pl
from jax.experimental.pallas import tpu as pltpu
from jax.sharding import PartitionSpec as P

LANES = 128
HALF = 64


def left_half(shape):
    return lax.broadcasted_iota(jnp.int32, shape, len(shape) - 1) < HALF


def gather_kernel(rows_ref, hubs_ref, xt_ref, out_ref, table_ref, *, peers, rows, hub_rows):
    step = pl.program_id(0)

    @pl.when(step == 0)
    def _():
        width = 512
        for c in range(xt_ref.shape[1] // width):
            part = xt_ref[:, c * width : (c + 1) * width]
            table_ref[c * width : (c + 1) * width, :] = jnp.concatenate([part, part], axis=0).T

    left = left_half((1, LANES))

    def pick(first, second):
        return jnp.where(left, table_ref[pl.ds(first, 1), :], table_ref[pl.ds(second, 1), :])

    def group(g, carry):
        peer = g // (rows // 8)
        row = (g % (rows // 8)) * 8
        base = (step * peers + peer) * 2 * rows + row
        picked = [pick(rows_ref[base + i], rows_ref[base + rows + i]) for i in range(8)]
        out_ref[peer, pl.ds(pl.multiple_of(row, 8), 8), :] = jnp.concatenate(picked, axis=0)
        return carry

    lax.fori_loop(0, peers * rows // 8, group, 0, unroll=2)

    for g in range(hub_rows // 8):
        picked = [pick(hubs_ref[g * 8 + i], hubs_ref[hub_rows + g * 8 + i]) for i in range(8)]
        block = jnp.concatenate(picked, axis=0)
        for peer in range(peers):
            out_ref[peer, rows + g * 8 : rows + g * 8 + 8, :] = block


def gather_rows(xt, send_rows, hub_list):
    peer_count = send_rows.shape[0]
    rows = send_rows.shape[1] // 2
    hub_rows = hub_list.shape[0] // 2
    peers = 8
    return pl.pallas_call(
        functools.partial(gather_kernel, peers=peers, rows=rows, hub_rows=hub_rows),
        grid_spec=pltpu.PrefetchScalarGridSpec(
            num_scalar_prefetch=2,
            grid=(peer_count // peers,),
            in_specs=[pl.BlockSpec(xt.shape, lambda i, *_: (0, 0))],
            out_specs=pl.BlockSpec((peers, rows + hub_rows, LANES), lambda i, *_: (i, 0, 0)),
            scratch_shapes=[pltpu.VMEM((xt.shape[1], LANES), jnp.float32)],
        ),
        out_shape=jax.ShapeDtypeStruct((peer_count, rows + hub_rows, LANES), jnp.float32),
        compiler_params=pltpu.CompilerParams(vmem_limit_bytes=24 * 2**20),
        cost_estimate=pl.CostEstimate(flops=10**7, bytes_accessed=4 * 2**20, transcendentals=0),
    )(send_rows.reshape(-1), hub_list, xt)


def split(value):
    high = value.astype(jnp.bfloat16)
    mid = (value - high.astype(jnp.float32)).astype(jnp.bfloat16)
    return high, mid


def split_kernel(tiles_ref, out_ref):
    for i in range(tiles_ref.shape[0]):
        high, mid = split(tiles_ref[i])
        out_ref[i, :, :LANES] = high
        out_ref[i, :, LANES:] = mid


def split_tiles(tile_vals):
    tiles, size, _ = tile_vals.shape
    step = 8
    return pl.pallas_call(
        split_kernel,
        grid=(tiles // step,),
        in_specs=[pl.BlockSpec((step, size, size), lambda i: (i, 0, 0))],
        out_specs=pl.BlockSpec((step, size, 2 * size), lambda i: (i, 0, 0)),
        out_shape=jax.ShapeDtypeStruct((tiles, size, 2 * size), jnp.bfloat16),
        compiler_params=pltpu.CompilerParams(vmem_limit_bytes=24 * 2**20),
        cost_estimate=pl.CostEstimate(flops=10**7, bytes_accessed=12 * 2**20, transcendentals=0),
    )(tile_vals)


def tile_kernel(src_ref, dst_ref, tiles_ref, mirror_ref, out_ref, acc_ref, *, rows, hub_rows, hub_tiles):
    step = pl.program_id(0)

    @pl.when(step == 0)
    def _():
        acc_ref[...] = jnp.zeros_like(acc_ref)

    count = tiles_ref.shape[0]
    left = left_half((rows, LANES))
    half = rows // 2
    for i in range(count):
        source = src_ref[step * count + i]
        is_hub = source < hub_tiles
        peer = jnp.where(is_hub, 2 * source, source - hub_tiles)
        other = jnp.where(is_hub, 2 * source + 1, source - hub_tiles)
        start = pl.multiple_of(jnp.where(is_hub, rows, 0), 8)
        middle = pl.multiple_of(jnp.where(is_hub, rows, half), 8)
        packed = jnp.concatenate(
            [mirror_ref[peer, pl.ds(start, half), :], mirror_ref[other, pl.ds(middle, half), :]], axis=0
        )
        swapped = pltpu.roll(packed, HALF, 1)
        low = jnp.where(left, packed, swapped)
        high = jnp.where(left, swapped, packed)
        second = jnp.where(is_hub, high[:half], low[half:])
        third = jnp.where(is_hub, low[half:], high[:half])
        block = jnp.concatenate([low[:half], second, third, high[half:]], axis=0)
        top, mid = split(block)
        right_side = jnp.concatenate(
            [jnp.concatenate([top, mid], axis=1), jnp.concatenate([mid, top], axis=1)], axis=0
        )
        product = jnp.dot(tiles_ref[i], right_side, preferred_element_type=jnp.float32)
        acc_ref[dst_ref[step * count + i]] += product[:, :LANES] + product[:, LANES:]

    @pl.when(step == pl.num_programs(0) - 1)
    def _():
        pick = left_half((8, LANES))
        for block in range(acc_ref.shape[0]):
            for part in range(8):
                first = acc_ref[block, part * 16 : part * 16 + 8, :]
                second = acc_ref[block, part * 16 + 8 : part * 16 + 16, :]
                out_ref[block * 8 + part] = jnp.where(pick, first, second)


def tile_stage(split_vals, mirror, tile_src, tile_dst, rows, hub_rows, hub_tiles, dst_blocks):
    tiles, size, _ = split_vals.shape
    step = 8
    return pl.pallas_call(
        functools.partial(tile_kernel, rows=rows, hub_rows=hub_rows, hub_tiles=hub_tiles),
        grid_spec=pltpu.PrefetchScalarGridSpec(
            num_scalar_prefetch=2,
            grid=(tiles // step,),
            in_specs=[
                pl.BlockSpec((step, size, 2 * size), lambda i, *_: (i, 0, 0)),
                pl.BlockSpec(mirror.shape, lambda i, *_: (0, 0, 0)),
            ],
            out_specs=pl.BlockSpec((dst_blocks * 8, 8, LANES), lambda i, *_: (0, 0, 0)),
            scratch_shapes=[pltpu.VMEM((dst_blocks, size, LANES), jnp.float32)],
        ),
        out_shape=jax.ShapeDtypeStruct((dst_blocks * 8, 8, LANES), jnp.float32),
        compiler_params=pltpu.CompilerParams(vmem_limit_bytes=32 * 2**20),
        cost_estimate=pl.CostEstimate(flops=10**9, bytes_accessed=10 * 2**20, transcendentals=0),
    )(tile_src, tile_dst, split_vals, mirror)


def slots_kernel(slots_ref, weights_ref, *out_refs):
    peers = slots_ref.shape[0]
    blocks = slots_ref.shape[1]
    gathered = jnp.concatenate(
        [slots_ref[:, k].reshape(peers * 8, LANES) for k in range(blocks)], axis=1
    )
    for d, out_ref in enumerate(out_refs):
        out_ref[...] = jnp.dot(
            gathered,
            weights_ref[d],
            precision=lax.Precision.HIGHEST,
            preferred_element_type=jnp.float32,
        )


def project_slots(slots, weights):
    peers, blocks = slots.shape[:2]
    return pl.pallas_call(
        slots_kernel,
        out_shape=[jax.ShapeDtypeStruct((peers * 8, LANES), jnp.float32)] * blocks,
        compiler_params=pltpu.CompilerParams(vmem_limit_bytes=24 * 2**20),
        cost_estimate=pl.CostEstimate(flops=10**9, bytes_accessed=3 * 2**20, transcendentals=0),
    )(slots, weights)


def scatter_kernel(rows_ref, *refs, blocks):
    parts = refs[:blocks]
    own_ref, bias_ref, out_ref = refs[blocks : blocks + 3]
    sums = refs[blocks + 3 :]
    for total in sums:
        total[...] = jnp.zeros_like(total)
    left = left_half((1, LANES))
    zero = jnp.zeros((1, LANES), jnp.float32)
    lanes = len(sums) // 2
    for d, part in enumerate(parts):
        count = part.shape[0]

        def add(g, carry, part=part, d=d, count=count):
            for i in range(lanes):
                row = g * lanes + i
                value = part[pl.ds(row, 1), :]
                first = rows_ref[(d * count + row) * 2]
                second = rows_ref[(d * count + row) * 2 + 1]
                sums[2 * i][pl.ds(first, 1), :] += jnp.where(left, value, zero)
                sums[2 * i + 1][pl.ds(second, 1), :] += jnp.where(left, zero, value)
            return carry

        lax.fori_loop(0, count // lanes, add, 0, unroll=8)
    width = 512
    for c in range(out_ref.shape[1] // width):
        columns = slice(c * width, (c + 1) * width)
        whole = functools.reduce(lambda a, b: a + b, [total[columns, :] for total in sums])
        turned = whole.T
        out_ref[:, columns] = jnp.maximum(
            turned[:HALF] + turned[HALF:] + own_ref[:, columns] + bias_ref[...], 0.0
        )


def scatter_rows(parts, rows, own, bias):
    return pl.pallas_call(
        functools.partial(scatter_kernel, blocks=len(parts)),
        in_specs=[pl.BlockSpec(memory_space=pltpu.SMEM)]
        + [pl.BlockSpec(memory_space=pltpu.VMEM)] * (len(parts) + 2),
        out_specs=pl.BlockSpec(memory_space=pltpu.VMEM),
        out_shape=jax.ShapeDtypeStruct(own.shape, jnp.float32),
        scratch_shapes=[pltpu.VMEM((own.shape[1] + 8, LANES), jnp.float32)] * 4,
        compiler_params=pltpu.CompilerParams(vmem_limit_bytes=32 * 2**20),
        cost_estimate=pl.CostEstimate(flops=10**7, bytes_accessed=4 * 2**20, transcendentals=0),
    )(rows, *parts, own, bias)


def shifted(value, count, step):
    return lax.ppermute(value, "feat", [(i, (i + step) % count) for i in range(count)])


def per_device(
    features,
    w_self,
    w_neigh,
    out_bias,
    hub_rows,
    replica_send_rows,
    ret_rows,
    tile_src,
    tile_dst,
    tile_vals,
    *,
    feat,
):
    xt = features.T
    peers, slot = replica_send_rows.shape[1:]
    ret = ret_rows.shape[2]
    outgoing = gather_rows(xt, replica_send_rows[0], hub_rows[0])
    mirror = lax.all_to_all(outgoing, "dom", split_axis=0, concat_axis=0, tiled=True)

    whole = lax.all_gather(xt, "feat", axis=0, tiled=True)
    own = lax.dot_general(
        w_self,
        whole,
        (((0,), (0,)), ((), ())),
        precision=lax.Precision.HIGHEST,
        preferred_element_type=jnp.float32,
    )
    split_vals = split_tiles(tile_vals[0])
    me = lax.axis_index("feat")
    weights = []
    for d in range(feat):
        mine = w_neigh if d == 0 else shifted(w_neigh, feat, -d)
        mine = mine.reshape(feat, HALF, HALF)
        empty = jnp.zeros_like(mine)
        weights.append(
            jnp.stack([jnp.concatenate([mine, empty], 2), jnp.concatenate([empty, mine], 2)], 1).reshape(
                feat * LANES, LANES
            )
        )
    weights = jnp.stack(weights)
    quarters = ret_rows[0].reshape(peers, feat, 2, 8).transpose(1, 0, 3, 2)
    order = jnp.stack(
        [lax.dynamic_index_in_dim(quarters, (me - d) % feat, 0, False) for d in range(feat)]
    ).reshape(-1)

    hub_tiles = hub_rows.shape[1] * peers // slot
    partial = tile_stage(
        split_vals,
        mirror,
        tile_src[0],
        tile_dst[0],
        slot // 2,
        hub_rows.shape[1] // 2,
        hub_tiles,
        peers * ret // slot,
    )
    slots = lax.all_to_all(partial, ("dom", "feat"), split_axis=0, concat_axis=0, tiled=True)
    parts = project_slots(slots.reshape(peers, feat, 8, LANES), weights)
    parts = [parts[0]] + [shifted(parts[d], feat, d) for d in range(1, feat)]
    return scatter_rows(parts, order, own, out_bias[:, None]).T


def solution(mesh):
    return jax.shard_map(
        functools.partial(per_device, feat=mesh.shape["feat"]),
        mesh=mesh,
        in_specs=(
            P("dom", "feat"),
            P(None, "feat"),
            P(None, "feat"),
            P("feat"),
            P("dom", None),
            P("dom", None, None),
            P("dom", None, None),
            P("dom", None),
            P("dom", None),
            P("dom", None, None, None),
        ),
        out_specs=P("dom", "feat"),
        check_vma=False,
    )
```

```python
import functools

import jax
import jax.numpy as jnp
from jax import lax
from jax.experimental import pallas as pl
from jax.experimental.pallas import tpu as pltpu
from jax.sharding import PartitionSpec as P

LANES = 128
KERNEL_VMEM = 50 * 2**20
HALF = 64


def left_half(shape):
    return lax.broadcasted_iota(jnp.int32, shape, len(shape) - 1) < HALF


def gather_kernel(rows_ref, hubs_ref, xt_hbm, out_ref, xt_ref, table_ref, hub_ref, sems, *, peers, rows, hub_rows):
    step = pl.program_id(0)
    chunks = sems.shape[0]
    width = xt_ref.shape[1] // chunks

    def fetch(c):
        columns = pl.ds(c * width, width)
        return pltpu.make_async_copy(xt_hbm.at[:, columns], xt_ref.at[:, columns], sems.at[c])

    @pl.when(step == 0)
    def _():
        for c in range(chunks):
            fetch(c).start()
        for c in range(chunks):
            fetch(c).wait()
            part = xt_ref[:, c * width : (c + 1) * width]
            table_ref[c * width : (c + 1) * width, :] = jnp.concatenate([part, part], axis=0).T

    left = left_half((1, LANES))

    def pick(first, second):
        return jnp.where(left, table_ref[pl.ds(first, 1), :], table_ref[pl.ds(second, 1), :])

    @pl.when(step == 0)
    def _():
        for half in range(2):
            start = half * 2 * hub_rows
            for i in range(hub_rows):
                hub_ref[half, i : i + 1, :] = pick(hubs_ref[start + i], hubs_ref[start + hub_rows + i])

    def one(peer, carry):
        base = (step * peers + peer) * 2 * rows
        for i in range(rows):
            out_ref[peer, i : i + 1, :] = pick(rows_ref[base + i], rows_ref[base + rows + i])
        out_ref[peer, rows : rows + hub_rows, :] = hub_ref[peer % 2]
        return carry

    lax.fori_loop(0, peers, one, 0)


def gather_rows(xt, send_rows, hub_list):
    peer_count = send_rows.shape[0]
    rows = send_rows.shape[1] // 2
    hub_rows = hub_list.shape[0] // 4
    peers = 8
    return pl.pallas_call(
        functools.partial(gather_kernel, peers=peers, rows=rows, hub_rows=hub_rows),
        grid_spec=pltpu.PrefetchScalarGridSpec(
            num_scalar_prefetch=2,
            grid=(peer_count // peers,),
            in_specs=[pl.BlockSpec(memory_space=pltpu.HBM)],
            out_specs=pl.BlockSpec((peers, rows + hub_rows, LANES), lambda i, *_: (i, 0, 0)),
            scratch_shapes=[
                pltpu.VMEM(xt.shape, jnp.float32),
                pltpu.VMEM((xt.shape[1], LANES), jnp.float32),
                pltpu.VMEM((2, hub_rows, LANES), jnp.float32),
                pltpu.SemaphoreType.DMA((8,)),
            ],
        ),
        out_shape=jax.ShapeDtypeStruct((peer_count, rows + hub_rows, LANES), jnp.float32),
        compiler_params=pltpu.CompilerParams(vmem_limit_bytes=60 * 2**20),
        cost_estimate=pl.CostEstimate(flops=10**7, bytes_accessed=4 * 2**20, transcendentals=0),
    )(send_rows.reshape(-1), hub_list, xt)


def split(value):
    high = value.astype(jnp.bfloat16)
    mid = (value - high.astype(jnp.float32)).astype(jnp.bfloat16)
    return high, mid


def split_kernel(src_ref, dst_ref, tiles_ref, out_ref, order_ref):
    count = tiles_ref.shape[0]
    for i in range(count):
        tile = pl.program_id(0) * count + i
        source = src_ref[tile]
        high, mid = split(tiles_ref[i])
        out_ref[source, :, :LANES] = high
        out_ref[source, :, LANES:] = mid
        order_ref[source] = dst_ref[tile]


def split_tiles(tile_vals, tile_src, tile_dst):
    tiles, size, _ = tile_vals.shape
    step = 8
    return pl.pallas_call(
        split_kernel,
        grid_spec=pltpu.PrefetchScalarGridSpec(
            num_scalar_prefetch=2,
            grid=(tiles // step,),
            in_specs=[pl.BlockSpec((step, size, size), lambda i, *_: (i, 0, 0))],
            out_specs=[
                pl.BlockSpec((tiles, size, 2 * size), lambda i, *_: (0, 0, 0)),
                pl.BlockSpec(memory_space=pltpu.SMEM),
            ],
        ),
        out_shape=[
            jax.ShapeDtypeStruct((tiles, size, 2 * size), jnp.bfloat16),
            jax.ShapeDtypeStruct((tiles,), jnp.int32),
        ],
        compiler_params=pltpu.CompilerParams(vmem_limit_bytes=40 * 2**20),
        cost_estimate=pl.CostEstimate(flops=10**7, bytes_accessed=12 * 2**20, transcendentals=0),
    )(tile_src, tile_dst, tile_vals)


def unpack(packed):
    left = left_half(packed.shape)
    swapped = pltpu.roll(packed, HALF, 1)
    return jnp.where(left, packed, swapped), jnp.where(left, swapped, packed)


def multiply(tile, block):
    top, mid = split(block)
    right_side = jnp.concatenate(
        [jnp.concatenate([top, mid], axis=1), jnp.concatenate([mid, top], axis=1)], axis=0
    )
    product = jnp.dot(tile, right_side, preferred_element_type=jnp.float32)
    return product[:, :LANES] + product[:, LANES:]


def packed_sums(acc_ref, block, part):
    first = acc_ref[block, part * 16 : part * 16 + 8, :]
    second = acc_ref[block, part * 16 + 8 : part * 16 + 16, :]
    return jnp.where(left_half((8, LANES)), first, second)


def listed_kernel(dst_ref, tiles_hbm, mirror_ref, out_ref, tiles_ref, acc_ref, sems, *, first, rows):
    chunks = sems.shape[0]
    count = tiles_ref.shape[0] // chunks

    def fetch(c):
        return pltpu.make_async_copy(
            tiles_hbm.at[pl.ds(first + c * count, count)], tiles_ref.at[pl.ds(c * count, count)], sems.at[c]
        )

    for c in range(chunks):
        fetch(c).start()
    acc_ref[...] = jnp.zeros_like(acc_ref)

    def chunk(c, carry):
        fetch(c).wait()
        for i in range(count):
            tile = c * count + i
            low, high = unpack(mirror_ref[tile, :rows, :])
            acc_ref[dst_ref[first + tile]] += multiply(tiles_ref[tile], jnp.concatenate([low, high], axis=0))
        return carry

    lax.fori_loop(0, chunks, chunk, 0)
    for block in range(acc_ref.shape[0]):
        for part in range(8):
            out_ref[block * 8 + part] = packed_sums(acc_ref, block, part)


def listed_tiles(split_vals, mirror, order, rows, first, dst_blocks):
    tiles, size, _ = split_vals.shape
    count = tiles - first
    whole = pl.BlockSpec(memory_space=pltpu.VMEM)
    return pl.pallas_call(
        functools.partial(listed_kernel, first=first, rows=rows),
        in_specs=[pl.BlockSpec(memory_space=pltpu.SMEM), pl.BlockSpec(memory_space=pltpu.HBM), whole],
        out_specs=whole,
        scratch_shapes=[
            pltpu.VMEM((count, size, 2 * size), jnp.bfloat16),
            pltpu.VMEM((dst_blocks, size, LANES), jnp.float32),
            pltpu.SemaphoreType.DMA((8,)),
        ],
        out_shape=jax.ShapeDtypeStruct((dst_blocks * 8, 8, LANES), jnp.float32),
        compiler_params=pltpu.CompilerParams(vmem_limit_bytes=KERNEL_VMEM),
        cost_estimate=pl.CostEstimate(flops=10**9, bytes_accessed=10 * 2**20, transcendentals=0),
    )(order, split_vals, mirror)


def hub_kernel(
    dst_ref, side_ref, tiles_hbm, own_ref, other_ref, before_ref, out_hbm, tiles_ref, hubs_ref, acc_ref, out_ref, sems, out_sems
):
    chunks = sems.shape[0]
    count = tiles_ref.shape[0] // chunks
    side = side_ref[0]

    def fetch(c):
        part = pl.ds(c * count, count)
        return pltpu.make_async_copy(tiles_hbm.at[part], tiles_ref.at[part], sems.at[c])

    for c in range(chunks):
        fetch(c).start()
    acc_ref[...] = jnp.zeros_like(acc_ref)
    hubs_ref[side] = own_ref[...]
    hubs_ref[1 - side] = other_ref[...]

    def chunk(c, carry):
        fetch(c).wait()
        for i in range(count):
            tile = c * count + i
            pieces = []
            for part in range(2):
                for half in range(2):
                    pieces.extend(unpack(hubs_ref[half, 2 * tile + part]))
            acc_ref[dst_ref[tile]] += multiply(tiles_ref[tile], jnp.concatenate(pieces, axis=0))
        return carry

    lax.fori_loop(0, chunks, chunk, 0)
    sends = out_sems.shape[0]
    blocks = acc_ref.shape[0] // sends
    results = []
    for c in range(sends):
        for block in range(c * blocks, (c + 1) * blocks):
            for part in range(8):
                out_ref[block * 8 + part] = packed_sums(acc_ref, block, part) + before_ref[block * 8 + part]
        span = pl.ds(c * blocks * 8, blocks * 8)
        results.append(pltpu.make_async_copy(out_ref.at[span], out_hbm.at[span], out_sems.at[c]))
        results[-1].start()
    for copy in results:
        copy.wait()


def hub_tiles(split_vals, own, other, before, order, side):
    _, size, _ = split_vals.shape
    blocks = before.shape[0] // 8
    scalars = pl.BlockSpec(memory_space=pltpu.SMEM)
    return pl.pallas_call(
        hub_kernel,
        in_specs=[scalars, scalars, pl.BlockSpec(memory_space=pltpu.HBM)]
        + [pl.BlockSpec(memory_space=pltpu.VMEM)] * 3,
        out_specs=pl.BlockSpec(memory_space=pltpu.HBM),
        scratch_shapes=[
            pltpu.VMEM((own.shape[0] // 2, size, 2 * size), jnp.bfloat16),
            pltpu.VMEM((2,) + own.shape, jnp.float32),
            pltpu.VMEM((blocks, size, LANES), jnp.float32),
            pltpu.VMEM(before.shape, jnp.float32),
            pltpu.SemaphoreType.DMA((4,)),
            pltpu.SemaphoreType.DMA((4,)),
        ],
        out_shape=jax.ShapeDtypeStruct(before.shape, jnp.float32),
        compiler_params=pltpu.CompilerParams(vmem_limit_bytes=KERNEL_VMEM),
        cost_estimate=pl.CostEstimate(flops=10**9, bytes_accessed=6 * 2**20, transcendentals=0),
    )(order, side, split_vals, own, other, before)


def weights_kernel(weights_ref, out_ref):
    for d in range(weights_ref.shape[0]):
        top, mid = split(weights_ref[d])
        depth = top.shape[0]
        out_ref[d, :depth, :LANES] = top
        out_ref[d, :depth, LANES:] = mid
        out_ref[d, depth:, :LANES] = mid
        out_ref[d, depth:, LANES:] = top


def split_weights(weights):
    count, depth, width = weights.shape
    return pl.pallas_call(
        weights_kernel,
        out_shape=jax.ShapeDtypeStruct((count, 2 * depth, 2 * width), jnp.bfloat16),
    )(weights)


def slots_kernel(slots_ref, weights_ref, *out_refs, targets):
    peers = slots_ref.shape[0]
    blocks = slots_ref.shape[1]
    tops, mids = [], []
    for k in range(blocks):
        top, mid = split(slots_ref[:, k].reshape(peers * 8, LANES))
        tops.append(top)
        mids.append(mid)
    whole = jnp.concatenate(tops + mids, axis=1)
    for d, out_ref in zip(targets, out_refs):
        product = jnp.dot(whole, weights_ref[d], preferred_element_type=jnp.float32)
        out_ref[...] = product[:, :LANES] + product[:, LANES:]


def project_slots(slots, weights, targets):
    peers = slots.shape[0]
    return pl.pallas_call(
        functools.partial(slots_kernel, targets=targets),
        out_shape=[jax.ShapeDtypeStruct((peers * 8, LANES), jnp.float32)] * len(targets),
        compiler_params=pltpu.CompilerParams(vmem_limit_bytes=24 * 2**20),
        cost_estimate=pl.CostEstimate(flops=10**7, bytes_accessed=16 * 2**20, transcendentals=0),
    )(slots, weights)


def scatter_kernel(rows_ref, *refs, blocks, last):
    parts = refs[:blocks]
    base_ref, bias_ref, out_ref = refs[blocks : blocks + 3]
    sums = refs[blocks + 3 :]
    for total in sums:
        total[...] = jnp.zeros_like(total)
    left = left_half((1, LANES))
    zero = jnp.zeros((1, LANES), jnp.float32)
    lanes = len(sums) // 2
    for d, part in enumerate(parts):
        count = part.shape[0]

        def add(g, carry, part=part, d=d, count=count):
            for i in range(lanes):
                row = g * lanes + i
                value = part[pl.ds(row, 1), :]
                first = rows_ref[(d * count + row) * 2]
                second = rows_ref[(d * count + row) * 2 + 1]
                sums[2 * i][pl.ds(first, 1), :] += jnp.where(left, value, zero)
                sums[2 * i + 1][pl.ds(second, 1), :] += jnp.where(left, zero, value)
            return carry

        lax.fori_loop(0, count // lanes, add, 0, unroll=8)
    width = 512
    for c in range(out_ref.shape[1] // width):
        columns = slice(c * width, (c + 1) * width)
        whole = functools.reduce(lambda a, b: a + b, [total[columns, :] for total in sums])
        turned = whole.T
        result = turned[:HALF] + turned[HALF:] + base_ref[:, columns]
        out_ref[:, columns] = jnp.maximum(result + bias_ref[...], 0.0) if last else result


def scatter_rows(parts, rows, base, bias, last):
    return pl.pallas_call(
        functools.partial(scatter_kernel, blocks=len(parts), last=last),
        in_specs=[pl.BlockSpec(memory_space=pltpu.SMEM)]
        + [pl.BlockSpec(memory_space=pltpu.VMEM)] * (len(parts) + 2),
        out_specs=pl.BlockSpec(memory_space=pltpu.VMEM),
        out_shape=jax.ShapeDtypeStruct(base.shape, jnp.float32),
        scratch_shapes=[pltpu.VMEM((base.shape[1] + 8, LANES), jnp.float32)] * 4,
        compiler_params=pltpu.CompilerParams(vmem_limit_bytes=16 * 2**20),
        cost_estimate=pl.CostEstimate(flops=10**7, bytes_accessed=16 * 2**20, transcendentals=0),
    )(rows, *parts, base, bias)


def shifted(value, count, step):
    return lax.ppermute(value, "feat", [(i, (i + step) % count) for i in range(count)])


def per_device(
    features,
    w_self,
    w_neigh,
    out_bias,
    hub_rows,
    replica_send_rows,
    ret_rows,
    tile_src,
    tile_dst,
    tile_vals,
    *,
    feat,
):
    xt = features.T
    peers, slot = replica_send_rows.shape[1:]
    ret = ret_rows.shape[2]
    outgoing = gather_rows(xt, replica_send_rows[0], hub_rows[0])
    mirror = lax.all_to_all(outgoing, "dom", split_axis=0, concat_axis=0, tiled=True)

    me = lax.axis_index("feat")
    width = xt.shape[0]
    neighbours = [w_neigh] + [shifted(w_neigh, feat, -d) for d in range(1, feat)]
    xt, tiles, neighbours = lax.optimization_barrier((xt, tile_vals[0], neighbours))
    blocks = [xt] + [shifted(xt, feat, d) for d in range(1, feat)]
    split_vals, tile_order = split_tiles(tiles, tile_src[0], tile_dst[0])

    mirror, split_vals, tile_order = lax.optimization_barrier((mirror, split_vals, tile_order))
    rows = slot // 2
    hub_count = hub_rows.shape[1] * peers // slot
    hub_half = mirror[:, rows:]
    hub_other = lax.ppermute(hub_half, "dom", [(i, i ^ 1) for i in range(peers)])
    side = (lax.axis_index("dom") % 2).astype(jnp.int32).reshape(1)
    partial = listed_tiles(split_vals, mirror, tile_order, rows, hub_count, peers * ret // slot)
    partial = hub_tiles(split_vals, hub_half, hub_other, partial, tile_order, side)
    partial, blocks, neighbours, w_self, ret_rows = lax.optimization_barrier(
        (partial, blocks, neighbours, w_self, ret_rows)
    )
    slots = lax.all_to_all(partial, ("dom", "feat"), split_axis=0, concat_axis=0, tiled=True)

    self_rows = w_self.reshape(feat, width, -1)
    self_rows = jnp.concatenate(
        [lax.dynamic_index_in_dim(self_rows, (me - d) % feat, 0, False) for d in range(feat)]
    )
    own = lax.dot_general(
        self_rows,
        jnp.concatenate(blocks),
        (((0,), (0,)), ((), ())),
        precision=lax.Precision.HIGHEST,
        preferred_element_type=jnp.float32,
    )
    weights = []
    for mine in neighbours:
        mine = mine.reshape(feat, width, width)
        empty = jnp.zeros_like(mine)
        weights.append(
            jnp.stack([jnp.concatenate([mine, empty], 2), jnp.concatenate([empty, mine], 2)], 1).reshape(
                feat * LANES, LANES
            )
        )
    weights = split_weights(jnp.stack(weights))
    quarters = ret_rows[0].reshape(peers, feat, 2, 8).transpose(1, 0, 3, 2)
    order = [
        lax.dynamic_index_in_dim(quarters, (me - d) % feat, 0, False).reshape(-1) for d in range(feat)
    ]
    far = feat // 2
    near = [d for d in range(feat - 1, 0, -1) if d != far]
    near_rows = jnp.concatenate([order[d] for d in near])
    bias = out_bias[:, None]
    slots, own, weights, near_rows, order, bias = lax.optimization_barrier(
        (slots, own, weights, near_rows, order, bias)
    )
    slots = slots.reshape(peers, feat, 8, LANES)
    parts = project_slots(slots, weights, range(feat))
    moved = {d: shifted(parts[d], feat, d) for d in near}
    total = scatter_rows([parts[0]], order[0], own, bias, False)
    last, total = lax.optimization_barrier((parts[far], total))
    moved[far] = shifted(last, feat, far)
    total = scatter_rows([moved[d] for d in near], near_rows, total, bias, False)
    return scatter_rows([moved[far]], order[far], total, bias, True).T


def solution(mesh):
    return jax.shard_map(
        functools.partial(per_device, feat=mesh.shape["feat"]),
        mesh=mesh,
        in_specs=(
            P("dom", "feat"),
            P(None, "feat"),
            P(None, "feat"),
            P("feat"),
            P("dom", None),
            P("dom", None, None),
            P("dom", None, None),
            P("dom", None),
            P("dom", None),
            P("dom", None, None, None),
        ),
        out_specs=P("dom", "feat"),
        check_vma=False,
    )
```

```python
import functools

import jax
import jax.numpy as jnp
from jax import lax
from jax.experimental import pallas as pl
from jax.experimental.pallas import tpu as pltpu
from jax.sharding import PartitionSpec as P

LANES = 128
KERNEL_VMEM = 50 * 2**20
HALF = 64


def left_half(shape):
    return lax.broadcasted_iota(jnp.int32, shape, len(shape) - 1) < HALF


def gather_kernel(rows_ref, hubs_ref, xt_hbm, out_ref, xt_ref, table_ref, hub_ref, sems, *, peers, rows, hub_rows):
    step = pl.program_id(0)
    chunks = sems.shape[0]
    width = xt_ref.shape[1] // chunks

    def fetch(c):
        columns = pl.ds(c * width, width)
        return pltpu.make_async_copy(xt_hbm.at[:, columns], xt_ref.at[:, columns], sems.at[c])

    @pl.when(step == 0)
    def _():
        for c in range(chunks):
            fetch(c).start()
        for c in range(chunks):
            fetch(c).wait()
            part = xt_ref[:, c * width : (c + 1) * width]
            table_ref[c * width : (c + 1) * width, :] = jnp.concatenate([part, part], axis=0).T

    left = left_half((1, LANES))

    def pick(first, second):
        return jnp.where(left, table_ref[pl.ds(first, 1), :], table_ref[pl.ds(second, 1), :])

    @pl.when(step == 0)
    def _():
        for half in range(2):
            start = half * 2 * hub_rows
            for i in range(hub_rows):
                hub_ref[half, i : i + 1, :] = pick(hubs_ref[start + i], hubs_ref[start + hub_rows + i])

    def one(peer, carry):
        base = (step * peers + peer) * 2 * rows
        for i in range(rows):
            out_ref[peer, i : i + 1, :] = pick(rows_ref[base + i], rows_ref[base + rows + i])
        out_ref[peer, rows : rows + hub_rows, :] = hub_ref[peer % 2]
        return carry

    lax.fori_loop(0, peers, one, 0)


def gather_rows(xt, send_rows, hub_list):
    peer_count = send_rows.shape[0]
    rows = send_rows.shape[1] // 2
    hub_rows = hub_list.shape[0] // 4
    peers = 8
    return pl.pallas_call(
        functools.partial(gather_kernel, peers=peers, rows=rows, hub_rows=hub_rows),
        grid_spec=pltpu.PrefetchScalarGridSpec(
            num_scalar_prefetch=2,
            grid=(peer_count // peers,),
            in_specs=[pl.BlockSpec(memory_space=pltpu.HBM)],
            out_specs=pl.BlockSpec((peers, rows + hub_rows, LANES), lambda i, *_: (i, 0, 0)),
            scratch_shapes=[
                pltpu.VMEM(xt.shape, jnp.float32),
                pltpu.VMEM((xt.shape[1], LANES), jnp.float32),
                pltpu.VMEM((2, hub_rows, LANES), jnp.float32),
                pltpu.SemaphoreType.DMA((8,)),
            ],
        ),
        out_shape=jax.ShapeDtypeStruct((peer_count, rows + hub_rows, LANES), jnp.float32),
        compiler_params=pltpu.CompilerParams(vmem_limit_bytes=60 * 2**20),
        cost_estimate=pl.CostEstimate(flops=10**7, bytes_accessed=4 * 2**20, transcendentals=0),
    )(send_rows.reshape(-1), hub_list, xt)


def split(value):
    high = value.astype(jnp.bfloat16)
    mid = (value - high.astype(jnp.float32)).astype(jnp.bfloat16)
    return high, mid


def split_kernel(src_ref, dst_ref, tiles_ref, out_ref, order_ref):
    count = tiles_ref.shape[0]
    for i in range(count):
        tile = pl.program_id(0) * count + i
        source = src_ref[tile]
        high, mid = split(tiles_ref[i])
        out_ref[source, :, :LANES] = high
        out_ref[source, :, LANES:] = mid
        order_ref[source] = dst_ref[tile]


def split_tiles(tile_vals, tile_src, tile_dst):
    tiles, size, _ = tile_vals.shape
    step = 8
    return pl.pallas_call(
        split_kernel,
        grid_spec=pltpu.PrefetchScalarGridSpec(
            num_scalar_prefetch=2,
            grid=(tiles // step,),
            in_specs=[pl.BlockSpec((step, size, size), lambda i, *_: (i, 0, 0))],
            out_specs=[
                pl.BlockSpec((tiles, size, 2 * size), lambda i, *_: (0, 0, 0)),
                pl.BlockSpec(memory_space=pltpu.SMEM),
            ],
        ),
        out_shape=[
            jax.ShapeDtypeStruct((tiles, size, 2 * size), jnp.bfloat16),
            jax.ShapeDtypeStruct((tiles,), jnp.int32),
        ],
        compiler_params=pltpu.CompilerParams(vmem_limit_bytes=40 * 2**20),
        cost_estimate=pl.CostEstimate(flops=10**7, bytes_accessed=12 * 2**20, transcendentals=0),
    )(tile_src, tile_dst, tile_vals)


def unpack(packed):
    left = left_half(packed.shape)
    swapped = pltpu.roll(packed, HALF, 1)
    return jnp.where(left, packed, swapped), jnp.where(left, swapped, packed)


def multiply(tile, block):
    top, mid = split(block)
    right_side = jnp.concatenate(
        [jnp.concatenate([top, mid], axis=1), jnp.concatenate([mid, top], axis=1)], axis=0
    )
    product = jnp.dot(tile, right_side, preferred_element_type=jnp.float32)
    return product[:, :LANES] + product[:, LANES:]


def packed_sums(acc_ref, block, part):
    first = acc_ref[block, part * 16 : part * 16 + 8, :]
    second = acc_ref[block, part * 16 + 8 : part * 16 + 16, :]
    return jnp.where(left_half((8, LANES)), first, second)


def listed_kernel(dst_ref, tiles_hbm, mirror_ref, out_ref, tiles_ref, acc_ref, sems, *, first, rows):
    chunks = sems.shape[0]
    count = tiles_ref.shape[0] // chunks

    def fetch(c):
        return pltpu.make_async_copy(
            tiles_hbm.at[pl.ds(first + c * count, count)], tiles_ref.at[pl.ds(c * count, count)], sems.at[c]
        )

    ahead = 2
    for c in range(ahead):
        fetch(c).start()
    acc_ref[...] = jnp.zeros_like(acc_ref)

    def chunk(c, carry):
        @pl.when(c + ahead < chunks)
        def _():
            fetch(c + ahead).start()

        fetch(c).wait()
        for i in range(count):
            tile = c * count + i
            low, high = unpack(mirror_ref[tile, :rows, :])
            acc_ref[dst_ref[first + tile]] += multiply(tiles_ref[tile], jnp.concatenate([low, high], axis=0))
        return carry

    lax.fori_loop(0, chunks, chunk, 0)
    for block in range(acc_ref.shape[0]):
        for part in range(8):
            out_ref[block * 8 + part] = packed_sums(acc_ref, block, part)


def listed_tiles(split_vals, mirror, order, rows, first, dst_blocks):
    tiles, size, _ = split_vals.shape
    count = tiles - first
    whole = pl.BlockSpec(memory_space=pltpu.VMEM)
    return pl.pallas_call(
        functools.partial(listed_kernel, first=first, rows=rows),
        in_specs=[pl.BlockSpec(memory_space=pltpu.SMEM), pl.BlockSpec(memory_space=pltpu.HBM), whole],
        out_specs=whole,
        scratch_shapes=[
            pltpu.VMEM((count, size, 2 * size), jnp.bfloat16),
            pltpu.VMEM((dst_blocks, size, LANES), jnp.float32),
            pltpu.SemaphoreType.DMA((8,)),
        ],
        out_shape=jax.ShapeDtypeStruct((dst_blocks * 8, 8, LANES), jnp.float32),
        compiler_params=pltpu.CompilerParams(vmem_limit_bytes=KERNEL_VMEM),
        cost_estimate=pl.CostEstimate(flops=10**9, bytes_accessed=10 * 2**20, transcendentals=0),
    )(order, split_vals, mirror)


def hub_kernel(
    dst_ref, side_ref, tiles_hbm, own_ref, other_ref, before_ref, out_hbm, tiles_ref, hubs_ref, acc_ref, out_ref, sems, out_sems
):
    chunks = sems.shape[0]
    count = tiles_ref.shape[0] // chunks
    side = side_ref[0]

    def fetch(c):
        part = pl.ds(c * count, count)
        return pltpu.make_async_copy(tiles_hbm.at[part], tiles_ref.at[part], sems.at[c])

    for c in range(chunks):
        fetch(c).start()
    acc_ref[...] = jnp.zeros_like(acc_ref)
    hubs_ref[side] = own_ref[...]
    hubs_ref[1 - side] = other_ref[...]

    def chunk(c, carry):
        fetch(c).wait()
        for i in range(count):
            tile = c * count + i
            pieces = []
            for part in range(2):
                for half in range(2):
                    pieces.extend(unpack(hubs_ref[half, 2 * tile + part]))
            acc_ref[dst_ref[tile]] += multiply(tiles_ref[tile], jnp.concatenate(pieces, axis=0))
        return carry

    lax.fori_loop(0, chunks, chunk, 0)
    sends = out_sems.shape[0]
    blocks = acc_ref.shape[0] // sends
    results = []
    for c in range(sends):
        for block in range(c * blocks, (c + 1) * blocks):
            for part in range(8):
                out_ref[block * 8 + part] = packed_sums(acc_ref, block, part) + before_ref[block * 8 + part]
        span = pl.ds(c * blocks * 8, blocks * 8)
        results.append(pltpu.make_async_copy(out_ref.at[span], out_hbm.at[span], out_sems.at[c]))
        results[-1].start()
    for copy in results:
        copy.wait()


def hub_tiles(split_vals, own, other, before, order, side):
    _, size, _ = split_vals.shape
    blocks = before.shape[0] // 8
    scalars = pl.BlockSpec(memory_space=pltpu.SMEM)
    return pl.pallas_call(
        hub_kernel,
        in_specs=[scalars, scalars, pl.BlockSpec(memory_space=pltpu.HBM)]
        + [pl.BlockSpec(memory_space=pltpu.VMEM)] * 3,
        out_specs=pl.BlockSpec(memory_space=pltpu.HBM),
        scratch_shapes=[
            pltpu.VMEM((own.shape[0] // 2, size, 2 * size), jnp.bfloat16),
            pltpu.VMEM((2,) + own.shape, jnp.float32),
            pltpu.VMEM((blocks, size, LANES), jnp.float32),
            pltpu.VMEM(before.shape, jnp.float32),
            pltpu.SemaphoreType.DMA((4,)),
            pltpu.SemaphoreType.DMA((4,)),
        ],
        out_shape=jax.ShapeDtypeStruct(before.shape, jnp.float32),
        compiler_params=pltpu.CompilerParams(vmem_limit_bytes=KERNEL_VMEM),
        cost_estimate=pl.CostEstimate(flops=10**9, bytes_accessed=6 * 2**20, transcendentals=0),
    )(order, side, split_vals, own, other, before)


def weights_kernel(weights_ref, out_ref):
    for d in range(weights_ref.shape[0]):
        top, mid = split(weights_ref[d])
        depth = top.shape[0]
        out_ref[d, :depth, :LANES] = top
        out_ref[d, :depth, LANES:] = mid
        out_ref[d, depth:, :LANES] = mid
        out_ref[d, depth:, LANES:] = top


def split_weights(weights):
    count, depth, width = weights.shape
    return pl.pallas_call(
        weights_kernel,
        out_shape=jax.ShapeDtypeStruct((count, 2 * depth, 2 * width), jnp.bfloat16),
    )(weights)


def slots_kernel(slots_ref, weights_ref, *out_refs, targets):
    peers = slots_ref.shape[0]
    blocks = slots_ref.shape[1]
    tops, mids = [], []
    for k in range(blocks):
        top, mid = split(slots_ref[:, k].reshape(peers * 8, LANES))
        tops.append(top)
        mids.append(mid)
    whole = jnp.concatenate(tops + mids, axis=1)
    for d, out_ref in zip(targets, out_refs):
        product = jnp.dot(whole, weights_ref[d], preferred_element_type=jnp.float32)
        out_ref[...] = product[:, :LANES] + product[:, LANES:]


def project_slots(slots, weights, targets):
    peers = slots.shape[0]
    return pl.pallas_call(
        functools.partial(slots_kernel, targets=targets),
        out_shape=[jax.ShapeDtypeStruct((peers * 8, LANES), jnp.float32)] * len(targets),
        compiler_params=pltpu.CompilerParams(vmem_limit_bytes=24 * 2**20),
        cost_estimate=pl.CostEstimate(flops=10**7, bytes_accessed=16 * 2**20, transcendentals=0),
    )(slots, weights)


def scatter_kernel(rows_ref, *refs, blocks, bases, last):
    parts = refs[:blocks]
    base_refs = refs[blocks : blocks + bases]
    bias_ref = refs[blocks + bases] if last else None
    out_ref, *sums = refs[blocks + bases + last :]
    for total in sums:
        total[...] = jnp.zeros_like(total)
    left = left_half((1, LANES))
    zero = jnp.zeros((1, LANES), jnp.float32)
    lanes = len(sums) // 2
    for d, part in enumerate(parts):
        count = part.shape[0]

        def add(g, carry, part=part, d=d, count=count):
            for i in range(lanes):
                row = g * lanes + i
                value = part[pl.ds(row, 1), :]
                first = rows_ref[(d * count + row) * 2]
                second = rows_ref[(d * count + row) * 2 + 1]
                sums[2 * i][pl.ds(first, 1), :] += jnp.where(left, value, zero)
                sums[2 * i + 1][pl.ds(second, 1), :] += jnp.where(left, zero, value)
            return carry

        lax.fori_loop(0, count // lanes, add, 0, unroll=8)
    width = 512
    for c in range(out_ref.shape[1] // width):
        columns = slice(c * width, (c + 1) * width)
        whole = functools.reduce(lambda a, b: a + b, [total[columns, :] for total in sums])
        turned = whole.T
        result = turned[:HALF] + turned[HALF:]
        for base in base_refs:
            result = result + base[:, columns]
        out_ref[:, columns] = jnp.maximum(result + bias_ref[...], 0.0) if last else result


def scatter_rows(parts, rows, bases, row_count, bias=None):
    last = bias is not None
    vmem = pl.BlockSpec(memory_space=pltpu.VMEM)
    return pl.pallas_call(
        functools.partial(scatter_kernel, blocks=len(parts), bases=len(bases), last=last),
        in_specs=[pl.BlockSpec(memory_space=pltpu.SMEM)] + [vmem] * (len(parts) + len(bases) + last),
        out_specs=vmem,
        out_shape=jax.ShapeDtypeStruct((HALF, row_count), jnp.float32),
        scratch_shapes=[pltpu.VMEM((row_count + 8, LANES), jnp.float32)] * 4,
        compiler_params=pltpu.CompilerParams(vmem_limit_bytes=16 * 2**20),
        cost_estimate=pl.CostEstimate(flops=10**7, bytes_accessed=16 * 2**20, transcendentals=0),
    )(rows, *parts, *bases, *([bias] if last else []))


def shifted(value, count, step):
    return lax.ppermute(value, "feat", [(i, (i + step) % count) for i in range(count)])


def per_device(
    features,
    w_self,
    w_neigh,
    out_bias,
    hub_rows,
    replica_send_rows,
    ret_rows,
    tile_src,
    tile_dst,
    tile_vals,
    *,
    feat,
):
    xt = features.T
    peers, slot = replica_send_rows.shape[1:]
    ret = ret_rows.shape[2]
    outgoing = gather_rows(xt, replica_send_rows[0], hub_rows[0])
    mirror = lax.all_to_all(outgoing, "dom", split_axis=0, concat_axis=0, tiled=True)

    me = lax.axis_index("feat")
    width = xt.shape[0]
    neighbours = [w_neigh] + [shifted(w_neigh, feat, -d) for d in range(1, feat)]
    xt, tiles, neighbours = lax.optimization_barrier((xt, tile_vals[0], neighbours))
    blocks = [xt] + [shifted(xt, feat, d) for d in range(1, feat)]
    split_vals, tile_order = split_tiles(tiles, tile_src[0], tile_dst[0])

    mirror, split_vals, tile_order = lax.optimization_barrier((mirror, split_vals, tile_order))
    rows = slot // 2
    hub_count = hub_rows.shape[1] * peers // slot
    hub_half = mirror[:, rows:]
    hub_other = lax.ppermute(hub_half, "dom", [(i, i ^ 1) for i in range(peers)])
    side = (lax.axis_index("dom") % 2).astype(jnp.int32).reshape(1)
    partial = listed_tiles(split_vals, mirror, tile_order, rows, hub_count, peers * ret // slot)
    partial = hub_tiles(split_vals, hub_half, hub_other, partial, tile_order, side)
    partial, blocks, neighbours, w_self, ret_rows = lax.optimization_barrier(
        (partial, blocks, neighbours, w_self, ret_rows)
    )
    slots = lax.all_to_all(partial, ("dom", "feat"), split_axis=0, concat_axis=0, tiled=True)

    self_rows = w_self.reshape(feat, width, -1)
    self_rows = jnp.concatenate(
        [lax.dynamic_index_in_dim(self_rows, (me - d) % feat, 0, False) for d in range(feat)]
    )
    own = lax.dot_general(
        self_rows,
        jnp.concatenate(blocks),
        (((0,), (0,)), ((), ())),
        precision=lax.Precision.HIGHEST,
        preferred_element_type=jnp.float32,
    )
    weights = []
    for mine in neighbours:
        mine = mine.reshape(feat, width, width)
        empty = jnp.zeros_like(mine)
        weights.append(
            jnp.stack([jnp.concatenate([mine, empty], 2), jnp.concatenate([empty, mine], 2)], 1).reshape(
                feat * LANES, LANES
            )
        )
    weights = split_weights(jnp.stack(weights))
    quarters = ret_rows[0].reshape(peers, feat, 2, 8).transpose(1, 0, 3, 2)
    order = [
        lax.dynamic_index_in_dim(quarters, (me - d) % feat, 0, False).reshape(-1) for d in range(feat)
    ]
    far = feat // 2
    near = [d for d in range(feat - 1, 0, -1) if d != far]
    tail = (*near[1:], far)
    tail_rows = jnp.concatenate([order[d] for d in tail])
    bias = out_bias[:, None]
    row_count = features.shape[0]
    slots, own, weights, tail_rows, order, bias = lax.optimization_barrier(
        (slots, own, weights, tail_rows, order, bias)
    )
    slots = slots.reshape(peers, feat, 8, LANES)
    parts = project_slots(slots, weights, range(feat))
    moved = {d: shifted(parts[d], feat, d) for d in near}
    total = scatter_rows([parts[0]], order[0], [], row_count)
    last, total = lax.optimization_barrier((parts[far], total))
    moved[far] = shifted(last, feat, far)
    total = scatter_rows([moved[near[0]]], order[near[0]], [total], row_count)
    return scatter_rows([moved[d] for d in tail], tail_rows, [total, own], row_count, bias).T


def solution(mesh):
    return jax.shard_map(
        functools.partial(per_device, feat=mesh.shape["feat"]),
        mesh=mesh,
        in_specs=(
            P("dom", "feat"),
            P(None, "feat"),
            P(None, "feat"),
            P("feat"),
            P("dom", None),
            P("dom", None, None),
            P("dom", None, None),
            P("dom", None),
            P("dom", None),
            P("dom", None, None, None),
        ),
        out_specs=P("dom", "feat"),
        check_vma=False,
    )
```

```python
import functools

import jax
import jax.numpy as jnp
from jax import lax
from jax.experimental import pallas as pl
from jax.experimental.pallas import tpu as pltpu
from jax.sharding import PartitionSpec as P

LANES = 128
KERNEL_VMEM = 48 * 2**20
HALF = 64


def left_half(shape):
    return lax.broadcasted_iota(jnp.int32, shape, len(shape) - 1) < HALF


def gather_kernel(rows_ref, hubs_ref, xt_hbm, out_ref, xt_ref, table_ref, hub_ref, sems, *, peers, rows, hub_rows):
    step = pl.program_id(0)
    chunks = sems.shape[0]
    width = xt_ref.shape[1] // chunks

    def fetch(c):
        columns = pl.ds(c * width, width)
        return pltpu.make_async_copy(xt_hbm.at[:, columns], xt_ref.at[:, columns], sems.at[c])

    @pl.when(step == 0)
    def _():
        for c in range(chunks):
            fetch(c).start()
        for c in range(chunks):
            fetch(c).wait()
            part = xt_ref[:, c * width : (c + 1) * width]
            table_ref[c * width : (c + 1) * width, :] = jnp.concatenate([part, part], axis=0).T

    left = left_half((1, LANES))

    def pick(first, second):
        return jnp.where(left, table_ref[pl.ds(first, 1), :], table_ref[pl.ds(second, 1), :])

    @pl.when(step == 0)
    def _():
        for half in range(2):
            start = half * 2 * hub_rows
            for i in range(hub_rows):
                hub_ref[half, i : i + 1, :] = pick(hubs_ref[start + i], hubs_ref[start + hub_rows + i])

    def one(peer, carry):
        base = (step * peers + peer) * 2 * rows
        for i in range(rows):
            out_ref[peer, i : i + 1, :] = pick(rows_ref[base + i], rows_ref[base + rows + i])
        out_ref[peer, rows : rows + hub_rows, :] = hub_ref[peer % 2]
        return carry

    lax.fori_loop(0, peers, one, 0)


def gather_rows(xt, send_rows, hub_list):
    peer_count = send_rows.shape[0]
    rows = send_rows.shape[1] // 2
    hub_rows = hub_list.shape[0] // 4
    peers = 8
    return pl.pallas_call(
        functools.partial(gather_kernel, peers=peers, rows=rows, hub_rows=hub_rows),
        grid_spec=pltpu.PrefetchScalarGridSpec(
            num_scalar_prefetch=2,
            grid=(peer_count // peers,),
            in_specs=[pl.BlockSpec(memory_space=pltpu.HBM)],
            out_specs=pl.BlockSpec((peers, rows + hub_rows, LANES), lambda i, *_: (i, 0, 0)),
            scratch_shapes=[
                pltpu.VMEM(xt.shape, jnp.float32),
                pltpu.VMEM((xt.shape[1], LANES), jnp.float32),
                pltpu.VMEM((2, hub_rows, LANES), jnp.float32),
                pltpu.SemaphoreType.DMA((8,)),
            ],
        ),
        out_shape=jax.ShapeDtypeStruct((peer_count, rows + hub_rows, LANES), jnp.float32),
        compiler_params=pltpu.CompilerParams(vmem_limit_bytes=60 * 2**20),
        cost_estimate=pl.CostEstimate(flops=10**7, bytes_accessed=4 * 2**20, transcendentals=0),
    )(send_rows.reshape(-1), hub_list, xt)


def split(value):
    high = value.astype(jnp.bfloat16)
    mid = (value - high.astype(jnp.float32)).astype(jnp.bfloat16)
    return high, mid


def split_kernel(src_ref, dst_ref, tiles_ref, out_ref, order_ref):
    count = tiles_ref.shape[0]
    for i in range(count):
        tile = pl.program_id(0) * count + i
        source = src_ref[tile]
        high, mid = split(tiles_ref[i])
        out_ref[source, :, :LANES] = high
        out_ref[source, :, LANES:] = mid
        order_ref[source] = dst_ref[tile]


def split_tiles(tile_vals, tile_src, tile_dst):
    tiles, size, _ = tile_vals.shape
    step = 8
    return pl.pallas_call(
        split_kernel,
        grid_spec=pltpu.PrefetchScalarGridSpec(
            num_scalar_prefetch=2,
            grid=(tiles // step,),
            in_specs=[pl.BlockSpec((step, size, size), lambda i, *_: (i, 0, 0))],
            out_specs=[
                pl.BlockSpec((tiles, size, 2 * size), lambda i, *_: (0, 0, 0)),
                pl.BlockSpec(memory_space=pltpu.SMEM),
            ],
        ),
        out_shape=[
            jax.ShapeDtypeStruct((tiles, size, 2 * size), jnp.bfloat16),
            jax.ShapeDtypeStruct((tiles,), jnp.int32),
        ],
        compiler_params=pltpu.CompilerParams(vmem_limit_bytes=40 * 2**20),
        cost_estimate=pl.CostEstimate(flops=10**7, bytes_accessed=12 * 2**20, transcendentals=0),
    )(tile_src, tile_dst, tile_vals)


def unpack(packed):
    left = left_half(packed.shape)
    swapped = pltpu.roll(packed, HALF, 1)
    return jnp.where(left, packed, swapped), jnp.where(left, swapped, packed)


def multiply(tile, block):
    top, mid = split(block)
    right_side = jnp.concatenate(
        [jnp.concatenate([top, mid], axis=1), jnp.concatenate([mid, top], axis=1)], axis=0
    )
    product = jnp.dot(tile, right_side, preferred_element_type=jnp.float32)
    return product[:, :LANES] + product[:, LANES:]


def packed_sums(acc_ref, block, part):
    first = acc_ref[block, part * 16 : part * 16 + 8, :]
    second = acc_ref[block, part * 16 + 8 : part * 16 + 16, :]
    return jnp.where(left_half((8, LANES)), first, second)


def listed_kernel(
    dst_ref, tiles_hbm, mirror_ref, out_ref, hub_tiles_ref, tiles_ref, acc_ref, sems, hub_sem, *, first, rows
):
    chunks = sems.shape[0]
    count = tiles_ref.shape[0] // chunks

    def fetch(c):
        return pltpu.make_async_copy(
            tiles_hbm.at[pl.ds(first + c * count, count)], tiles_ref.at[pl.ds(c * count, count)], sems.at[c]
        )

    for c in range(chunks):
        fetch(c).start()
    hubs = pltpu.make_async_copy(tiles_hbm.at[pl.ds(0, first)], hub_tiles_ref, hub_sem)
    hubs.start()
    acc_ref[...] = jnp.zeros_like(acc_ref)

    def chunk(c, carry):
        fetch(c).wait()
        for i in range(count):
            tile = c * count + i
            low, high = unpack(mirror_ref[tile, :rows, :])
            acc_ref[dst_ref[first + tile]] += multiply(tiles_ref[tile], jnp.concatenate([low, high], axis=0))
        return carry

    lax.fori_loop(0, chunks, chunk, 0)
    for block in range(acc_ref.shape[0]):
        for part in range(8):
            out_ref[block * 8 + part] = packed_sums(acc_ref, block, part)
    hubs.wait()


def listed_tiles(split_vals, mirror, order, rows, first, dst_blocks):
    tiles, size, _ = split_vals.shape
    count = tiles - first
    whole = pl.BlockSpec(memory_space=pltpu.VMEM)
    return pl.pallas_call(
        functools.partial(listed_kernel, first=first, rows=rows),
        in_specs=[pl.BlockSpec(memory_space=pltpu.SMEM), pl.BlockSpec(memory_space=pltpu.HBM), whole],
        out_specs=[whole, whole],
        scratch_shapes=[
            pltpu.VMEM((count, size, 2 * size), jnp.bfloat16),
            pltpu.VMEM((dst_blocks, size, LANES), jnp.float32),
            pltpu.SemaphoreType.DMA((8,)),
            pltpu.SemaphoreType.DMA,
        ],
        out_shape=[
            jax.ShapeDtypeStruct((dst_blocks * 8, 8, LANES), jnp.float32),
            jax.ShapeDtypeStruct((first, size, 2 * size), jnp.bfloat16),
        ],
        compiler_params=pltpu.CompilerParams(vmem_limit_bytes=KERNEL_VMEM),
        cost_estimate=pl.CostEstimate(flops=10**9, bytes_accessed=10 * 2**20, transcendentals=0),
    )(order, split_vals, mirror)


def hub_kernel(
    dst_ref, side_ref, tiles_ref, own_ref, other_ref, before_ref, out_hbm, hubs_ref, acc_ref, out_ref, out_sems
):
    count = 8
    chunks = tiles_ref.shape[0] // count
    side = side_ref[0]
    acc_ref[...] = jnp.zeros_like(acc_ref)
    hubs_ref[side] = own_ref[...]
    hubs_ref[1 - side] = other_ref[...]

    def chunk(c, carry):
        for i in range(count):
            tile = c * count + i
            pieces = []
            for part in range(2):
                for half in range(2):
                    pieces.extend(unpack(hubs_ref[half, 2 * tile + part]))
            acc_ref[dst_ref[tile]] += multiply(tiles_ref[tile], jnp.concatenate(pieces, axis=0))
        return carry

    lax.fori_loop(0, chunks, chunk, 0)
    sends = out_sems.shape[0]
    blocks = acc_ref.shape[0] // sends
    results = []
    for c in range(sends):
        for block in range(c * blocks, (c + 1) * blocks):
            for part in range(8):
                out_ref[block * 8 + part] = packed_sums(acc_ref, block, part) + before_ref[block * 8 + part]
        span = pl.ds(c * blocks * 8, blocks * 8)
        results.append(pltpu.make_async_copy(out_ref.at[span], out_hbm.at[span], out_sems.at[c]))
        results[-1].start()
    for copy in results:
        copy.wait()


def hub_tiles(split_vals, own, other, before, order, side):
    _, size, _ = split_vals.shape
    blocks = before.shape[0] // 8
    scalars = pl.BlockSpec(memory_space=pltpu.SMEM)
    return pl.pallas_call(
        hub_kernel,
        in_specs=[scalars, scalars] + [pl.BlockSpec(memory_space=pltpu.VMEM)] * 4,
        out_specs=pl.BlockSpec(memory_space=pltpu.HBM),
        scratch_shapes=[
            pltpu.VMEM((2,) + own.shape, jnp.float32),
            pltpu.VMEM((blocks, size, LANES), jnp.float32),
            pltpu.VMEM(before.shape, jnp.float32),
            pltpu.SemaphoreType.DMA((4,)),
        ],
        out_shape=jax.ShapeDtypeStruct(before.shape, jnp.float32),
        compiler_params=pltpu.CompilerParams(vmem_limit_bytes=KERNEL_VMEM),
        cost_estimate=pl.CostEstimate(flops=10**9, bytes_accessed=6 * 2**20, transcendentals=0),
    )(order, side, split_vals, own, other, before)


def weights_kernel(weights_ref, out_ref):
    for d in range(weights_ref.shape[0]):
        top, mid = split(weights_ref[d])
        depth = top.shape[0]
        out_ref[d, :depth, :LANES] = top
        out_ref[d, :depth, LANES:] = mid
        out_ref[d, depth:, :LANES] = mid
        out_ref[d, depth:, LANES:] = top


def split_weights(weights):
    count, depth, width = weights.shape
    return pl.pallas_call(
        weights_kernel,
        out_shape=jax.ShapeDtypeStruct((count, 2 * depth, 2 * width), jnp.bfloat16),
    )(weights)


def slots_kernel(slots_ref, weights_ref, *out_refs, targets):
    peers = slots_ref.shape[0]
    blocks = slots_ref.shape[1]
    tops, mids = [], []
    for k in range(blocks):
        top, mid = split(slots_ref[:, k].reshape(peers * 8, LANES))
        tops.append(top)
        mids.append(mid)
    whole = jnp.concatenate(tops + mids, axis=1)
    for d, out_ref in zip(targets, out_refs):
        product = jnp.dot(whole, weights_ref[d], preferred_element_type=jnp.float32)
        out_ref[...] = product[:, :LANES] + product[:, LANES:]


def project_slots(slots, weights, targets):
    peers = slots.shape[0]
    return pl.pallas_call(
        functools.partial(slots_kernel, targets=targets),
        out_shape=[jax.ShapeDtypeStruct((peers * 8, LANES), jnp.float32)] * len(targets),
        compiler_params=pltpu.CompilerParams(vmem_limit_bytes=12 * 2**20),
        cost_estimate=pl.CostEstimate(flops=10**7, bytes_accessed=16 * 2**20, transcendentals=0),
    )(slots, weights)


def scatter_kernel(rows_ref, *refs, blocks, bases, last):
    parts = refs[:blocks]
    base_refs = refs[blocks : blocks + bases]
    bias_ref = refs[blocks + bases] if last else None
    out_ref, *sums = refs[blocks + bases + last :]
    for total in sums:
        total[...] = jnp.zeros_like(total)
    left = left_half((1, LANES))
    zero = jnp.zeros((1, LANES), jnp.float32)
    lanes = len(sums) // 2
    for d, part in enumerate(parts):
        count = part.shape[0]

        def add(g, carry, part=part, d=d, count=count):
            for i in range(lanes):
                row = g * lanes + i
                value = part[pl.ds(row, 1), :]
                first = rows_ref[(d * count + row) * 2]
                second = rows_ref[(d * count + row) * 2 + 1]
                sums[2 * i][pl.ds(first, 1), :] += jnp.where(left, value, zero)
                sums[2 * i + 1][pl.ds(second, 1), :] += jnp.where(left, zero, value)
            return carry

        lax.fori_loop(0, count // lanes, add, 0, unroll=8)
    width = 512
    for c in range(out_ref.shape[1] // width):
        columns = slice(c * width, (c + 1) * width)
        whole = functools.reduce(lambda a, b: a + b, [total[columns, :] for total in sums])
        turned = whole.T
        result = turned[:HALF] + turned[HALF:]
        for base in base_refs:
            result = result + base[:, columns]
        out_ref[:, columns] = jnp.maximum(result + bias_ref[...], 0.0) if last else result


def scatter_rows(parts, rows, bases, row_count, bias=None):
    last = bias is not None
    vmem = pl.BlockSpec(memory_space=pltpu.VMEM)
    return pl.pallas_call(
        functools.partial(scatter_kernel, blocks=len(parts), bases=len(bases), last=last),
        in_specs=[pl.BlockSpec(memory_space=pltpu.SMEM)] + [vmem] * (len(parts) + len(bases) + last),
        out_specs=vmem,
        out_shape=jax.ShapeDtypeStruct((HALF, row_count), jnp.float32),
        scratch_shapes=[pltpu.VMEM((row_count + 8, LANES), jnp.float32)] * 4,
        compiler_params=pltpu.CompilerParams(vmem_limit_bytes=13 * 2**20),
        cost_estimate=pl.CostEstimate(flops=10**7, bytes_accessed=16 * 2**20, transcendentals=0),
    )(rows, *parts, *bases, *([bias] if last else []))


def shifted(value, count, step):
    return lax.ppermute(value, "feat", [(i, (i + step) % count) for i in range(count)])


def per_device(
    features,
    w_self,
    w_neigh,
    out_bias,
    hub_rows,
    replica_send_rows,
    ret_rows,
    tile_src,
    tile_dst,
    tile_vals,
    *,
    feat,
):
    xt = features.T
    peers, slot = replica_send_rows.shape[1:]
    ret = ret_rows.shape[2]
    outgoing = gather_rows(xt, replica_send_rows[0], hub_rows[0])
    mirror = lax.all_to_all(outgoing, "dom", split_axis=0, concat_axis=0, tiled=True)

    me = lax.axis_index("feat")
    width = xt.shape[0]
    neighbours = [w_neigh] + [shifted(w_neigh, feat, -d) for d in range(1, feat)]
    xt, tiles, neighbours = lax.optimization_barrier((xt, tile_vals[0], neighbours))
    blocks = [xt] + [shifted(xt, feat, d) for d in range(1, feat)]
    split_vals, tile_order = split_tiles(tiles, tile_src[0], tile_dst[0])

    mirror, split_vals, tile_order = lax.optimization_barrier((mirror, split_vals, tile_order))
    rows = slot // 2
    hub_count = hub_rows.shape[1] * peers // slot
    hub_half = mirror[:, rows:]
    hub_other = lax.ppermute(hub_half, "dom", [(i, i ^ 1) for i in range(peers)])
    side = (lax.axis_index("dom") % 2).astype(jnp.int32).reshape(1)
    partial, hub_vals = listed_tiles(split_vals, mirror, tile_order, rows, hub_count, peers * ret // slot)
    partial = hub_tiles(hub_vals, hub_half, hub_other, partial, tile_order, side)
    partial, blocks, neighbours, w_self, ret_rows = lax.optimization_barrier(
        (partial, blocks, neighbours, w_self, ret_rows)
    )
    slots = lax.all_to_all(partial, ("dom", "feat"), split_axis=0, concat_axis=0, tiled=True)

    self_rows = w_self.reshape(feat, width, -1)
    self_rows = jnp.concatenate(
        [lax.dynamic_index_in_dim(self_rows, (me - d) % feat, 0, False) for d in range(feat)]
    )
    own = lax.dot_general(
        self_rows,
        jnp.concatenate(blocks),
        (((0,), (0,)), ((), ())),
        precision=lax.Precision.HIGHEST,
        preferred_element_type=jnp.float32,
    )
    weights = []
    for mine in neighbours:
        mine = mine.reshape(feat, width, width)
        empty = jnp.zeros_like(mine)
        weights.append(
            jnp.stack([jnp.concatenate([mine, empty], 2), jnp.concatenate([empty, mine], 2)], 1).reshape(
                feat * LANES, LANES
            )
        )
    weights = split_weights(jnp.stack(weights))
    quarters = ret_rows[0].reshape(peers, feat, 2, 8).transpose(1, 0, 3, 2)
    order = [
        lax.dynamic_index_in_dim(quarters, (me - d) % feat, 0, False).reshape(-1) for d in range(feat)
    ]
    far = feat // 2
    near = [d for d in range(feat - 1, 0, -1) if d != far]
    tail = (far, *near)
    tail_rows = jnp.concatenate([order[d] for d in tail])
    bias = out_bias[:, None]
    row_count = features.shape[0]
    slots, own, weights, tail_rows, order, bias = lax.optimization_barrier(
        (slots, own, weights, tail_rows, order, bias)
    )
    slots = slots.reshape(peers, feat, 8, LANES)
    parts = project_slots(slots, weights, range(feat))
    moved = {d: shifted(parts[d], feat, d) for d in tail}
    total = scatter_rows([parts[0]], order[0], [own], row_count)
    return scatter_rows([moved[d] for d in tail], tail_rows, [total], row_count, bias).T


def solution(mesh):
    return jax.shard_map(
        functools.partial(per_device, feat=mesh.shape["feat"]),
        mesh=mesh,
        in_specs=(
            P("dom", "feat"),
            P(None, "feat"),
            P(None, "feat"),
            P("feat"),
            P("dom", None),
            P("dom", None, None),
            P("dom", None, None),
            P("dom", None),
            P("dom", None),
            P("dom", None, None, None),
        ),
        out_specs=P("dom", "feat"),
        check_vma=False,
    )
```

```python
import functools

import jax
import jax.numpy as jnp
from jax import lax
from jax.experimental import pallas as pl
from jax.experimental.pallas import tpu as pltpu
from jax.sharding import PartitionSpec as P

LANES = 128
KERNEL_VMEM = 48 * 2**20
HALF = 64


def left_half(shape):
    return lax.broadcasted_iota(jnp.int32, shape, len(shape) - 1) < HALF


def gather_kernel(
    rows_hbm, hubs_hbm, xt_hbm, out_hbm, rows_ref, hubs_ref, xt_ref, table_ref, hub_ref, out_ref, sems, list_sems, out_sems,
    *, rows, hub_rows
):
    lists = [
        pltpu.make_async_copy(rows_hbm, rows_ref, list_sems.at[0]),
        pltpu.make_async_copy(hubs_hbm, hubs_ref, list_sems.at[1]),
    ]
    for copy in lists:
        copy.start()
    chunks = sems.shape[0]
    width = xt_ref.shape[1] // chunks

    def fetch(c):
        columns = pl.ds(c * width, width)
        return pltpu.make_async_copy(xt_hbm.at[:, columns], xt_ref.at[:, columns], sems.at[c])

    for c in range(chunks):
        fetch(c).start()
    for c in range(chunks):
        fetch(c).wait()
        part = xt_ref[:, c * width : (c + 1) * width]
        table_ref[c * width : (c + 1) * width, :] = jnp.concatenate([part, part], axis=0).T
    for copy in lists:
        copy.wait()

    left = left_half((1, LANES))

    def pick(first, second):
        return jnp.where(left, table_ref[pl.ds(first, 1), :], table_ref[pl.ds(second, 1), :])

    for half in range(2):
        start = half * 2 * hub_rows
        for i in range(hub_rows):
            hub_ref[half, i : i + 1, :] = pick(hubs_ref[start + i], hubs_ref[start + hub_rows + i])

    def one(peer, carry):
        base = peer * 2 * rows
        for i in range(rows):
            out_ref[peer, i : i + 1, :] = pick(rows_ref[base + i], rows_ref[base + rows + i])
        out_ref[peer, rows : rows + hub_rows, :] = hub_ref[lax.rem(peer, 2)]
        return carry

    groups = out_sems.shape[0]
    peers = out_ref.shape[0] // groups

    def send(g):
        span = pl.ds(g * peers, peers)
        return pltpu.make_async_copy(out_ref.at[span], out_hbm.at[span], out_sems.at[g])

    def group(g, carry):
        lax.fori_loop(g * peers, (g + 1) * peers, one, 0)
        send(g).start()
        return carry

    lax.fori_loop(0, groups, group, 0)
    for g in range(groups):
        send(g).wait()


def gather_rows(xt, send_rows, hub_list):
    peer_count = send_rows.shape[0]
    rows = send_rows.shape[1] // 2
    hub_rows = hub_list.shape[0] // 4
    shape = (peer_count, rows + hub_rows, LANES)
    return pl.pallas_call(
        functools.partial(gather_kernel, rows=rows, hub_rows=hub_rows),
        in_specs=[pl.BlockSpec(memory_space=pltpu.HBM)] * 3,
        out_specs=pl.BlockSpec(memory_space=pltpu.HBM),
        scratch_shapes=[
            pltpu.SMEM((send_rows.size,), jnp.int32),
            pltpu.SMEM(hub_list.shape, jnp.int32),
            pltpu.VMEM(xt.shape, jnp.float32),
            pltpu.VMEM((xt.shape[1], LANES), jnp.float32),
            pltpu.VMEM((2, hub_rows, LANES), jnp.float32),
            pltpu.VMEM(shape, jnp.float32),
            pltpu.SemaphoreType.DMA((8,)),
            pltpu.SemaphoreType.DMA((2,)),
            pltpu.SemaphoreType.DMA((16,)),
        ],
        out_shape=jax.ShapeDtypeStruct(shape, jnp.float32),
        compiler_params=pltpu.CompilerParams(vmem_limit_bytes=60 * 2**20),
        cost_estimate=pl.CostEstimate(flops=10**7, bytes_accessed=4 * 2**20, transcendentals=0),
    )(send_rows.reshape(-1), hub_list, xt)


def split(value):
    high = value.astype(jnp.bfloat16)
    mid = (value - high.astype(jnp.float32)).astype(jnp.bfloat16)
    return high, mid


def split_kernel(src_ref, dst_ref, tiles_ref, out_ref, order_ref):
    count = tiles_ref.shape[0]
    for i in range(count):
        tile = pl.program_id(0) * count + i
        source = src_ref[tile]
        high, mid = split(tiles_ref[i])
        out_ref[source, :, :LANES] = high
        out_ref[source, :, LANES:] = mid
        order_ref[source] = dst_ref[tile]


def split_tiles(tile_vals, tile_src, tile_dst):
    tiles, size, _ = tile_vals.shape
    step = 8
    return pl.pallas_call(
        split_kernel,
        grid_spec=pltpu.PrefetchScalarGridSpec(
            num_scalar_prefetch=2,
            grid=(tiles // step,),
            in_specs=[pl.BlockSpec((step, size, size), lambda i, *_: (i, 0, 0))],
            out_specs=[
                pl.BlockSpec((tiles, size, 2 * size), lambda i, *_: (0, 0, 0)),
                pl.BlockSpec(memory_space=pltpu.SMEM),
            ],
        ),
        out_shape=[
            jax.ShapeDtypeStruct((tiles, size, 2 * size), jnp.bfloat16),
            jax.ShapeDtypeStruct((tiles,), jnp.int32),
        ],
        compiler_params=pltpu.CompilerParams(vmem_limit_bytes=40 * 2**20),
        cost_estimate=pl.CostEstimate(flops=10**7, bytes_accessed=12 * 2**20, transcendentals=0),
    )(tile_src, tile_dst, tile_vals)


def unpack(packed):
    left = left_half(packed.shape)
    swapped = pltpu.roll(packed, HALF, 1)
    return jnp.where(left, packed, swapped), jnp.where(left, swapped, packed)


def multiply(tile, block):
    top, mid = split(block)
    right_side = jnp.concatenate(
        [jnp.concatenate([top, mid], axis=1), jnp.concatenate([mid, top], axis=1)], axis=0
    )
    product = jnp.dot(tile, right_side, preferred_element_type=jnp.float32)
    return product[:, :LANES] + product[:, LANES:]


def packed_sums(acc_ref, block, part):
    first = acc_ref[block, part * 16 : part * 16 + 8, :]
    second = acc_ref[block, part * 16 + 8 : part * 16 + 16, :]
    return jnp.where(left_half((8, LANES)), first, second)


def listed_kernel(
    dst_ref, tiles_hbm, mirror_ref, out_ref, hub_tiles_ref, tiles_ref, acc_ref, sems, hub_sem, *, first, rows
):
    chunks = sems.shape[0]
    count = tiles_ref.shape[0] // chunks

    def fetch(c):
        return pltpu.make_async_copy(
            tiles_hbm.at[pl.ds(first + c * count, count)], tiles_ref.at[pl.ds(c * count, count)], sems.at[c]
        )

    piece = count // 4
    for c in range(chunks * 4):
        pltpu.make_async_copy(
            tiles_hbm.at[pl.ds(first + c * piece, piece)], tiles_ref.at[pl.ds(c * piece, piece)], sems.at[c // 4]
        ).start()
    hubs = pltpu.make_async_copy(tiles_hbm.at[pl.ds(0, first)], hub_tiles_ref, hub_sem)
    hubs.start()
    acc_ref[...] = jnp.zeros_like(acc_ref)

    def chunk(c, carry):
        fetch(c).wait()
        for i in range(count):
            tile = c * count + i
            low, high = unpack(mirror_ref[tile, :rows, :])
            acc_ref[dst_ref[first + tile]] += multiply(tiles_ref[tile], jnp.concatenate([low, high], axis=0))
        return carry

    lax.fori_loop(0, chunks, chunk, 0)
    for block in range(acc_ref.shape[0]):
        for part in range(8):
            out_ref[block * 8 + part] = packed_sums(acc_ref, block, part)
    hubs.wait()


def listed_tiles(split_vals, mirror, order, rows, first, dst_blocks):
    tiles, size, _ = split_vals.shape
    count = tiles - first
    whole = pl.BlockSpec(memory_space=pltpu.VMEM)
    return pl.pallas_call(
        functools.partial(listed_kernel, first=first, rows=rows),
        in_specs=[pl.BlockSpec(memory_space=pltpu.SMEM), pl.BlockSpec(memory_space=pltpu.HBM), whole],
        out_specs=[whole, whole],
        scratch_shapes=[
            pltpu.VMEM((count, size, 2 * size), jnp.bfloat16),
            pltpu.VMEM((dst_blocks, size, LANES), jnp.float32),
            pltpu.SemaphoreType.DMA((8,)),
            pltpu.SemaphoreType.DMA,
        ],
        out_shape=[
            jax.ShapeDtypeStruct((dst_blocks * 8, 8, LANES), jnp.float32),
            jax.ShapeDtypeStruct((first, size, 2 * size), jnp.bfloat16),
        ],
        compiler_params=pltpu.CompilerParams(vmem_limit_bytes=KERNEL_VMEM),
        cost_estimate=pl.CostEstimate(flops=10**9, bytes_accessed=10 * 2**20, transcendentals=0),
    )(order, split_vals, mirror)


def hub_kernel(
    dst_ref, side_ref, tiles_ref, own_ref, other_ref, before_ref, out_hbm, hubs_ref, acc_ref, out_ref, out_sems
):
    count = 8
    chunks = tiles_ref.shape[0] // count
    side = side_ref[0]
    acc_ref[...] = jnp.zeros_like(acc_ref)
    hubs_ref[side] = own_ref[...]
    hubs_ref[1 - side] = other_ref[...]

    def chunk(c, carry):
        for i in range(count):
            tile = c * count + i
            pieces = []
            for part in range(2):
                for half in range(2):
                    pieces.extend(unpack(hubs_ref[half, 2 * tile + part]))
            acc_ref[dst_ref[tile]] += multiply(tiles_ref[tile], jnp.concatenate(pieces, axis=0))
        return carry

    lax.fori_loop(0, chunks, chunk, 0)
    sends = out_sems.shape[0]
    blocks = acc_ref.shape[0] // sends
    results = []
    for c in range(sends):
        for block in range(c * blocks, (c + 1) * blocks):
            for part in range(8):
                out_ref[block * 8 + part] = packed_sums(acc_ref, block, part) + before_ref[block * 8 + part]
        span = pl.ds(c * blocks * 8, blocks * 8)
        results.append(pltpu.make_async_copy(out_ref.at[span], out_hbm.at[span], out_sems.at[c]))
        results[-1].start()
    for copy in results:
        copy.wait()


def hub_tiles(split_vals, own, other, before, order, side):
    _, size, _ = split_vals.shape
    blocks = before.shape[0] // 8
    scalars = pl.BlockSpec(memory_space=pltpu.SMEM)
    return pl.pallas_call(
        hub_kernel,
        in_specs=[scalars, scalars] + [pl.BlockSpec(memory_space=pltpu.VMEM)] * 4,
        out_specs=pl.BlockSpec(memory_space=pltpu.HBM),
        scratch_shapes=[
            pltpu.VMEM((2,) + own.shape, jnp.float32),
            pltpu.VMEM((blocks, size, LANES), jnp.float32),
            pltpu.VMEM(before.shape, jnp.float32),
            pltpu.SemaphoreType.DMA((4,)),
        ],
        out_shape=jax.ShapeDtypeStruct(before.shape, jnp.float32),
        compiler_params=pltpu.CompilerParams(vmem_limit_bytes=KERNEL_VMEM),
        cost_estimate=pl.CostEstimate(flops=10**9, bytes_accessed=6 * 2**20, transcendentals=0),
    )(order, side, split_vals, own, other, before)


def weights_kernel(weights_ref, out_ref):
    for d in range(weights_ref.shape[0]):
        top, mid = split(weights_ref[d])
        depth = top.shape[0]
        out_ref[d, :depth, :LANES] = top
        out_ref[d, :depth, LANES:] = mid
        out_ref[d, depth:, :LANES] = mid
        out_ref[d, depth:, LANES:] = top


def split_weights(weights):
    count, depth, width = weights.shape
    return pl.pallas_call(
        weights_kernel,
        out_shape=jax.ShapeDtypeStruct((count, 2 * depth, 2 * width), jnp.bfloat16),
    )(weights)


def slots_kernel(slots_ref, weights_ref, kept_ref, *refs, targets):
    moved = len(targets)
    out_refs, (held_ref, sems) = refs[:moved], refs[moved:]
    peers = slots_ref.shape[0]
    blocks = slots_ref.shape[1]
    tops, mids = [], []
    for k in range(blocks):
        top, mid = split(slots_ref[:, k].reshape(peers * 8, LANES))
        tops.append(top)
        mids.append(mid)
    whole = jnp.concatenate(tops + mids, axis=1)

    def product(d):
        both = jnp.dot(whole, weights_ref[d], preferred_element_type=jnp.float32)
        return both[:, :LANES] + both[:, LANES:]

    copies = []
    for i, d in enumerate(targets):
        held_ref[i] = product(d)
        copies.append(pltpu.make_async_copy(held_ref.at[i], out_refs[i], sems.at[i]))
        copies[-1].start()
    kept_ref[...] = product(0)
    for copy in copies:
        copy.wait()


def project_slots(slots, weights, targets):
    peers = slots.shape[0]
    moved = len(targets)
    shape = jax.ShapeDtypeStruct((peers * 8, LANES), jnp.float32)
    vmem = pl.BlockSpec(memory_space=pltpu.VMEM)
    return pl.pallas_call(
        functools.partial(slots_kernel, targets=targets),
        in_specs=[vmem, vmem],
        out_specs=[vmem] + [pl.BlockSpec(memory_space=pltpu.HBM)] * moved,
        out_shape=[shape] * (moved + 1),
        scratch_shapes=[
            pltpu.VMEM((moved,) + shape.shape, jnp.float32),
            pltpu.SemaphoreType.DMA((moved,)),
        ],
        compiler_params=pltpu.CompilerParams(vmem_limit_bytes=12 * 2**20),
        cost_estimate=pl.CostEstimate(flops=10**7, bytes_accessed=4 * 2**20, transcendentals=0),
    )(slots, weights)


def scatter_kernel(rows_ref, *refs, blocks, bases, last):
    parts = refs[:blocks]
    base_refs = refs[blocks : blocks + bases]
    bias_ref = refs[blocks + bases] if last else None
    refs = refs[blocks + bases + last :]
    if last:
        out_hbm, *sums, out_ref, sems = refs
    else:
        out_ref, *sums = refs
    for total in sums:
        total[...] = jnp.zeros_like(total)
    left = left_half((1, LANES))
    zero = jnp.zeros((1, LANES), jnp.float32)
    lanes = len(sums) // 2
    for d, part in enumerate(parts):
        count = part.shape[0]

        def add(g, carry, part=part, d=d, count=count):
            for i in range(lanes):
                row = g * lanes + i
                value = part[pl.ds(row, 1), :]
                first = rows_ref[(d * count + row) * 2]
                second = rows_ref[(d * count + row) * 2 + 1]
                sums[2 * i][pl.ds(first, 1), :] += jnp.where(left, value, zero)
                sums[2 * i + 1][pl.ds(second, 1), :] += jnp.where(left, zero, value)
            return carry

        lax.fori_loop(0, count // lanes, add, 0, unroll=8)
    width = 512
    copies = []
    for c in range(out_ref.shape[1] // width):
        columns = slice(c * width, (c + 1) * width)
        whole = functools.reduce(lambda a, b: a + b, [total[columns, :] for total in sums])
        turned = whole.T
        result = turned[:HALF] + turned[HALF:]
        for base in base_refs:
            result = result + base[:, columns]
        out_ref[:, columns] = jnp.maximum(result + bias_ref[...], 0.0) if last else result
        if last:
            copies.append(pltpu.make_async_copy(out_ref.at[:, columns], out_hbm.at[:, columns], sems.at[c]))
            copies[-1].start()
    for copy in copies:
        copy.wait()


def scatter_rows(parts, rows, bases, row_count, bias=None):
    last = bias is not None
    vmem = pl.BlockSpec(memory_space=pltpu.VMEM)
    return pl.pallas_call(
        functools.partial(scatter_kernel, blocks=len(parts), bases=len(bases), last=last),
        in_specs=[pl.BlockSpec(memory_space=pltpu.SMEM)] + [vmem] * (len(parts) + len(bases) + last),
        out_specs=pl.BlockSpec(memory_space=pltpu.HBM) if last else vmem,
        out_shape=jax.ShapeDtypeStruct((HALF, row_count), jnp.float32),
        scratch_shapes=[pltpu.VMEM((row_count + 8, LANES), jnp.float32)] * 4
        + ([pltpu.VMEM((HALF, row_count), jnp.float32), pltpu.SemaphoreType.DMA((8,))] if last else []),
        compiler_params=pltpu.CompilerParams(vmem_limit_bytes=13 * 2**20),
        cost_estimate=pl.CostEstimate(flops=10**7, bytes_accessed=16 * 2**20, transcendentals=0),
    )(rows, *parts, *bases, *([bias] if last else []))


def shifted(value, count, step):
    return lax.ppermute(value, "feat", [(i, (i + step) % count) for i in range(count)])


def per_device(
    features,
    w_self,
    w_neigh,
    out_bias,
    hub_rows,
    replica_send_rows,
    ret_rows,
    tile_src,
    tile_dst,
    tile_vals,
    *,
    feat,
):
    xt = features.T
    peers, slot = replica_send_rows.shape[1:]
    ret = ret_rows.shape[2]
    outgoing = gather_rows(xt, replica_send_rows[0], hub_rows[0])
    mirror = lax.all_to_all(outgoing, "dom", split_axis=0, concat_axis=0, tiled=True)

    me = lax.axis_index("feat")
    width = xt.shape[0]
    neighbours = [w_neigh] + [shifted(w_neigh, feat, -d) for d in range(1, feat)]
    xt, tiles, neighbours = lax.optimization_barrier((xt, tile_vals[0], neighbours))
    blocks = [xt] + [shifted(xt, feat, d) for d in range(1, feat)]
    split_vals, tile_order = split_tiles(tiles, tile_src[0], tile_dst[0])

    mirror, split_vals, tile_order = lax.optimization_barrier((mirror, split_vals, tile_order))
    rows = slot // 2
    hub_count = hub_rows.shape[1] * peers // slot
    hub_half = mirror[:, rows:]
    hub_other = lax.ppermute(hub_half, "dom", [(i, i ^ 1) for i in range(peers)])
    side = (lax.axis_index("dom") % 2).astype(jnp.int32).reshape(1)
    partial, hub_vals = listed_tiles(split_vals, mirror, tile_order, rows, hub_count, peers * ret // slot)
    partial = hub_tiles(hub_vals, hub_half, hub_other, partial, tile_order, side)
    partial, blocks, neighbours, w_self, ret_rows = lax.optimization_barrier(
        (partial, blocks, neighbours, w_self, ret_rows)
    )
    slots = lax.all_to_all(partial, ("dom", "feat"), split_axis=0, concat_axis=0, tiled=True)

    self_rows = w_self.reshape(feat, width, -1)
    self_rows = jnp.concatenate(
        [lax.dynamic_index_in_dim(self_rows, (me - d) % feat, 0, False) for d in range(feat)]
    )
    own = lax.dot_general(
        self_rows,
        jnp.concatenate(blocks),
        (((0,), (0,)), ((), ())),
        precision=lax.Precision.HIGHEST,
        preferred_element_type=jnp.float32,
    )
    weights = []
    for mine in neighbours:
        mine = mine.reshape(feat, width, width)
        empty = jnp.zeros_like(mine)
        weights.append(
            jnp.stack([jnp.concatenate([mine, empty], 2), jnp.concatenate([empty, mine], 2)], 1).reshape(
                feat * LANES, LANES
            )
        )
    weights = split_weights(jnp.stack(weights))
    quarters = ret_rows[0].reshape(peers, feat, 2, 8).transpose(1, 0, 3, 2)
    order = [
        lax.dynamic_index_in_dim(quarters, (me - d) % feat, 0, False).reshape(-1) for d in range(feat)
    ]
    far = feat // 2
    near = [d for d in range(feat - 1, 0, -1) if d != far]
    near_rows = jnp.concatenate([order[d] for d in near])
    bias = out_bias[:, None]
    row_count = features.shape[0]
    slots, own, weights, near_rows, order, bias = lax.optimization_barrier(
        (slots, own, weights, near_rows, order, bias)
    )
    slots = slots.reshape(peers, feat, 8, LANES)
    targets = (far, *near)
    kept, *parts = project_slots(slots, weights, targets)
    moved = {d: shifted(part, feat, d) for d, part in zip(targets, parts)}
    total = scatter_rows([kept], order[0], [own], row_count)
    total = scatter_rows([moved[far]], order[far], [total], row_count)
    return scatter_rows([moved[d] for d in near], near_rows, [total], row_count, bias).T


def solution(mesh):
    return jax.shard_map(
        functools.partial(per_device, feat=mesh.shape["feat"]),
        mesh=mesh,
        in_specs=(
            P("dom", "feat"),
            P(None, "feat"),
            P(None, "feat"),
            P("feat"),
            P("dom", None),
            P("dom", None, None),
            P("dom", None, None),
            P("dom", None),
            P("dom", None),
            P("dom", None, None, None),
        ),
        out_specs=P("dom", "feat"),
        check_vma=False,
    )
```

```python
import functools

import jax
import jax.numpy as jnp
from jax import lax
from jax.experimental import pallas as pl
from jax.experimental.pallas import tpu as pltpu
from jax.sharding import PartitionSpec as P

LANES = 128
KERNEL_VMEM = 46 * 2**20
HALF = 64


def left_half(shape):
    return lax.broadcasted_iota(jnp.int32, shape, len(shape) - 1) < HALF


def gather_kernel(
    rows_hbm, hubs_hbm, xt_hbm, out_hbm, rows_ref, hubs_ref, xt_ref, table_ref, hub_ref, out_ref, sems, list_sems, out_sems,
    *, rows, hub_rows
):
    lists = [
        pltpu.make_async_copy(rows_hbm, rows_ref, list_sems.at[0]),
        pltpu.make_async_copy(hubs_hbm, hubs_ref, list_sems.at[1]),
    ]
    for copy in lists:
        copy.start()
    chunks = sems.shape[0]
    width = xt_ref.shape[1] // chunks

    def fetch(c):
        columns = pl.ds(c * width, width)
        return pltpu.make_async_copy(xt_hbm.at[:, columns], xt_ref.at[:, columns], sems.at[c])

    for c in range(chunks):
        fetch(c).start()
    for c in range(chunks):
        fetch(c).wait()
        part = xt_ref[:, c * width : (c + 1) * width]
        table_ref[c * width : (c + 1) * width, :] = jnp.concatenate([part, part], axis=0).T
    for copy in lists:
        copy.wait()

    left = left_half((1, LANES))

    def pick(first, second):
        return jnp.where(left, table_ref[pl.ds(first, 1), :], table_ref[pl.ds(second, 1), :])

    for half in range(2):
        start = half * 2 * hub_rows
        for i in range(hub_rows):
            hub_ref[half, i : i + 1, :] = pick(hubs_ref[start + i], hubs_ref[start + hub_rows + i])

    def one(peer, carry):
        base = peer * 2 * rows
        for i in range(rows):
            out_ref[peer, i : i + 1, :] = pick(rows_ref[base + i], rows_ref[base + rows + i])
        out_ref[peer, rows : rows + hub_rows, :] = hub_ref[lax.rem(peer, 2)]
        return carry

    groups = out_sems.shape[0]
    peers = out_ref.shape[0] // groups

    def send(g):
        span = pl.ds(g * peers, peers)
        return pltpu.make_async_copy(out_ref.at[span], out_hbm.at[span], out_sems.at[g])

    def group(g, carry):
        lax.fori_loop(g * peers, (g + 1) * peers, one, 0)
        send(g).start()
        return carry

    lax.fori_loop(0, groups, group, 0)
    for g in range(groups):
        send(g).wait()


def gather_rows(xt, send_rows, hub_list):
    peer_count = send_rows.shape[0]
    rows = send_rows.shape[1] // 2
    hub_rows = hub_list.shape[0] // 4
    shape = (peer_count, rows + hub_rows, LANES)
    return pl.pallas_call(
        functools.partial(gather_kernel, rows=rows, hub_rows=hub_rows),
        in_specs=[pl.BlockSpec(memory_space=pltpu.HBM)] * 3,
        out_specs=pl.BlockSpec(memory_space=pltpu.HBM),
        scratch_shapes=[
            pltpu.SMEM((send_rows.size,), jnp.int32),
            pltpu.SMEM(hub_list.shape, jnp.int32),
            pltpu.VMEM(xt.shape, jnp.float32),
            pltpu.VMEM((xt.shape[1], LANES), jnp.float32),
            pltpu.VMEM((2, hub_rows, LANES), jnp.float32),
            pltpu.VMEM(shape, jnp.float32),
            pltpu.SemaphoreType.DMA((8,)),
            pltpu.SemaphoreType.DMA((2,)),
            pltpu.SemaphoreType.DMA((16,)),
        ],
        out_shape=jax.ShapeDtypeStruct(shape, jnp.float32),
        compiler_params=pltpu.CompilerParams(vmem_limit_bytes=60 * 2**20),
        cost_estimate=pl.CostEstimate(flops=10**7, bytes_accessed=4 * 2**20, transcendentals=0),
    )(send_rows.reshape(-1), hub_list, xt)


def split(value):
    high = value.astype(jnp.bfloat16)
    mid = (value - high.astype(jnp.float32)).astype(jnp.bfloat16)
    return high, mid


def split_kernel(src_ref, dst_ref, tiles_ref, out_ref, order_ref):
    count = tiles_ref.shape[0]
    for i in range(count):
        tile = pl.program_id(0) * count + i
        source = src_ref[tile]
        high, mid = split(tiles_ref[i])
        out_ref[source, :, :LANES] = high
        out_ref[source, :, LANES:] = mid
        order_ref[source] = dst_ref[tile]


def split_tiles(tile_vals, tile_src, tile_dst):
    tiles, size, _ = tile_vals.shape
    step = 8
    return pl.pallas_call(
        split_kernel,
        grid_spec=pltpu.PrefetchScalarGridSpec(
            num_scalar_prefetch=2,
            grid=(tiles // step,),
            in_specs=[pl.BlockSpec((step, size, size), lambda i, *_: (i, 0, 0))],
            out_specs=[
                pl.BlockSpec((tiles, size, 2 * size), lambda i, *_: (0, 0, 0)),
                pl.BlockSpec(memory_space=pltpu.SMEM),
            ],
        ),
        out_shape=[
            jax.ShapeDtypeStruct((tiles, size, 2 * size), jnp.bfloat16),
            jax.ShapeDtypeStruct((tiles,), jnp.int32),
        ],
        compiler_params=pltpu.CompilerParams(vmem_limit_bytes=40 * 2**20),
        cost_estimate=pl.CostEstimate(flops=10**7, bytes_accessed=12 * 2**20, transcendentals=0),
    )(tile_src, tile_dst, tile_vals)


def unpack(packed):
    left = left_half(packed.shape)
    swapped = pltpu.roll(packed, HALF, 1)
    return jnp.where(left, packed, swapped), jnp.where(left, swapped, packed)


def multiply(tile, block):
    left = left_half(block.shape)
    top = block.astype(jnp.bfloat16).astype(jnp.float32)
    mid = block - top
    right_side = jnp.concatenate(
        [jnp.where(left, top, mid).astype(jnp.bfloat16), jnp.where(left, mid, top).astype(jnp.bfloat16)], axis=0
    )
    product = jnp.dot(tile, right_side, preferred_element_type=jnp.float32)
    return product + pltpu.roll(product, HALF, 1)


def packed_sums(acc_ref, block, part):
    first = acc_ref[block, part * 16 : part * 16 + 8, :]
    second = acc_ref[block, part * 16 + 8 : part * 16 + 16, :]
    return jnp.where(left_half((8, LANES)), first, second)


def listed_kernel(
    dst_ref, tiles_hbm, mirror_ref, acc_ref, hub_tiles_ref, tiles_ref, sems, hub_sem, *, first, rows
):
    chunks = sems.shape[0]
    count = tiles_ref.shape[0] // chunks

    def fetch(c):
        return pltpu.make_async_copy(
            tiles_hbm.at[pl.ds(first + c * count, count)], tiles_ref.at[pl.ds(c * count, count)], sems.at[c]
        )

    piece = count // 4
    for c in range(chunks * 4):
        pltpu.make_async_copy(
            tiles_hbm.at[pl.ds(first + c * piece, piece)], tiles_ref.at[pl.ds(c * piece, piece)], sems.at[c // 4]
        ).start()
    hubs = pltpu.make_async_copy(tiles_hbm.at[pl.ds(0, first)], hub_tiles_ref, hub_sem)
    hubs.start()
    acc_ref[...] = jnp.zeros_like(acc_ref)

    def chunk(c, carry):
        fetch(c).wait()
        for i in range(count):
            tile = c * count + i
            low, high = unpack(mirror_ref[tile, :rows, :])
            acc_ref[dst_ref[first + tile]] += multiply(tiles_ref[tile], jnp.concatenate([low, high], axis=0))
        return carry

    lax.fori_loop(0, chunks, chunk, 0)
    hubs.wait()


def listed_tiles(split_vals, mirror, order, rows, first, dst_blocks):
    tiles, size, _ = split_vals.shape
    count = tiles - first
    whole = pl.BlockSpec(memory_space=pltpu.VMEM)
    return pl.pallas_call(
        functools.partial(listed_kernel, first=first, rows=rows),
        in_specs=[pl.BlockSpec(memory_space=pltpu.SMEM), pl.BlockSpec(memory_space=pltpu.HBM), whole],
        out_specs=[whole, whole],
        scratch_shapes=[
            pltpu.VMEM((count, size, 2 * size), jnp.bfloat16),
            pltpu.SemaphoreType.DMA((8,)),
            pltpu.SemaphoreType.DMA,
        ],
        out_shape=[
            jax.ShapeDtypeStruct((dst_blocks, size, LANES), jnp.float32),
            jax.ShapeDtypeStruct((first, size, 2 * size), jnp.bfloat16),
        ],
        compiler_params=pltpu.CompilerParams(vmem_limit_bytes=KERNEL_VMEM),
        cost_estimate=pl.CostEstimate(flops=10**9, bytes_accessed=10 * 2**20, transcendentals=0),
    )(order, split_vals, mirror)


def hub_kernel(
    dst_ref, side_ref, tiles_ref, own_ref, other_ref, before_ref, out_hbm, hubs_ref, acc_ref, out_ref, out_sems
):
    count = 8
    chunks = tiles_ref.shape[0] // count
    side = side_ref[0]
    acc_ref[...] = before_ref[...]
    hubs_ref[side] = own_ref[...]
    hubs_ref[1 - side] = other_ref[...]

    def chunk(c, carry):
        for i in range(count):
            tile = c * count + i
            pieces = []
            for part in range(2):
                for half in range(2):
                    pieces.extend(unpack(hubs_ref[half, 2 * tile + part]))
            acc_ref[dst_ref[tile]] += multiply(tiles_ref[tile], jnp.concatenate(pieces, axis=0))
        return carry

    lax.fori_loop(0, chunks, chunk, 0)
    sends = out_sems.shape[0]
    blocks = acc_ref.shape[0] // sends
    results = []
    for c in range(sends):
        for block in range(c * blocks, (c + 1) * blocks):
            for part in range(8):
                out_ref[block * 8 + part] = packed_sums(acc_ref, block, part)
        span = pl.ds(c * blocks * 8, blocks * 8)
        results.append(pltpu.make_async_copy(out_ref.at[span], out_hbm.at[span], out_sems.at[c]))
        results[-1].start()
    for copy in results:
        copy.wait()


def hub_tiles(split_vals, own, other, before, order, side):
    blocks, size, _ = before.shape
    scalars = pl.BlockSpec(memory_space=pltpu.SMEM)
    result = jax.ShapeDtypeStruct((blocks * 8, 8, LANES), jnp.float32)
    return pl.pallas_call(
        hub_kernel,
        in_specs=[scalars, scalars] + [pl.BlockSpec(memory_space=pltpu.VMEM)] * 4,
        out_specs=pl.BlockSpec(memory_space=pltpu.HBM),
        scratch_shapes=[
            pltpu.VMEM((2,) + own.shape, jnp.float32),
            pltpu.VMEM(before.shape, jnp.float32),
            pltpu.VMEM(result.shape, jnp.float32),
            pltpu.SemaphoreType.DMA((4,)),
        ],
        out_shape=result,
        compiler_params=pltpu.CompilerParams(vmem_limit_bytes=KERNEL_VMEM),
        cost_estimate=pl.CostEstimate(flops=10**9, bytes_accessed=6 * 2**20, transcendentals=0),
    )(order, side, split_vals, own, other, before)


def weights_kernel(weights_ref, out_ref):
    for d in range(weights_ref.shape[0]):
        top, mid = split(weights_ref[d])
        depth = top.shape[0]
        out_ref[d, :depth, :LANES] = top
        out_ref[d, :depth, LANES:] = mid
        out_ref[d, depth:, :LANES] = mid
        out_ref[d, depth:, LANES:] = top


def split_weights(weights):
    count, depth, width = weights.shape
    return pl.pallas_call(
        weights_kernel,
        out_shape=jax.ShapeDtypeStruct((count, 2 * depth, 2 * width), jnp.bfloat16),
    )(weights)


def slots_kernel(slots_ref, weights_ref, kept_ref, *refs, targets):
    moved = len(targets)
    out_refs, (held_ref, sems) = refs[:moved], refs[moved:]
    peers = slots_ref.shape[0]
    blocks = slots_ref.shape[1]
    tops, mids = [], []
    for k in range(blocks):
        top, mid = split(slots_ref[:, k].reshape(peers * 8, LANES))
        tops.append(top)
        mids.append(mid)
    whole = jnp.concatenate(tops + mids, axis=1)

    def product(d):
        both = jnp.dot(whole, weights_ref[d], preferred_element_type=jnp.float32)
        return both[:, :LANES] + both[:, LANES:]

    copies = []
    for i, d in enumerate(targets):
        held_ref[i] = product(d)
        copies.append(pltpu.make_async_copy(held_ref.at[i], out_refs[i], sems.at[i]))
        copies[-1].start()
    kept_ref[...] = product(0)
    for copy in copies:
        copy.wait()


def project_slots(slots, weights, targets):
    peers = slots.shape[0]
    moved = len(targets)
    shape = jax.ShapeDtypeStruct((peers * 8, LANES), jnp.float32)
    vmem = pl.BlockSpec(memory_space=pltpu.VMEM)
    return pl.pallas_call(
        functools.partial(slots_kernel, targets=targets),
        in_specs=[vmem, vmem],
        out_specs=[vmem] + [pl.BlockSpec(memory_space=pltpu.HBM)] * moved,
        out_shape=[shape] * (moved + 1),
        scratch_shapes=[
            pltpu.VMEM((moved,) + shape.shape, jnp.float32),
            pltpu.SemaphoreType.DMA((moved,)),
        ],
        compiler_params=pltpu.CompilerParams(vmem_limit_bytes=12 * 2**20),
        cost_estimate=pl.CostEstimate(flops=10**7, bytes_accessed=4 * 2**20, transcendentals=0),
    )(slots, weights)


def scatter_kernel(rows_ref, *refs, blocks, bases, last):
    parts = refs[:blocks]
    base_refs = refs[blocks : blocks + bases]
    bias_ref = refs[blocks + bases] if last else None
    refs = refs[blocks + bases + last :]
    if last:
        out_hbm, *sums, out_ref, sems = refs
    else:
        out_ref, *sums = refs
    for total in sums:
        total[...] = jnp.zeros_like(total)
    left = left_half((1, LANES))
    zero = jnp.zeros((1, LANES), jnp.float32)
    lanes = len(sums) // 2
    for d, part in enumerate(parts):
        count = part.shape[0]

        def add(g, carry, part=part, d=d, count=count):
            for i in range(lanes):
                row = g * lanes + i
                value = part[pl.ds(row, 1), :]
                first = rows_ref[(d * count + row) * 2]
                second = rows_ref[(d * count + row) * 2 + 1]
                sums[2 * i][pl.ds(first, 1), :] += jnp.where(left, value, zero)
                sums[2 * i + 1][pl.ds(second, 1), :] += jnp.where(left, zero, value)
            return carry

        lax.fori_loop(0, count // lanes, add, 0, unroll=8)
    width = 512
    copies = []
    for c in range(out_ref.shape[1] // width):
        columns = slice(c * width, (c + 1) * width)
        whole = functools.reduce(lambda a, b: a + b, [total[columns, :] for total in sums])
        turned = whole.T
        result = turned[:HALF] + turned[HALF:]
        for base in base_refs:
            result = result + base[:, columns]
        out_ref[:, columns] = jnp.maximum(result + bias_ref[...], 0.0) if last else result
        if last:
            copies.append(pltpu.make_async_copy(out_ref.at[:, columns], out_hbm.at[:, columns], sems.at[c]))
            copies[-1].start()
    for copy in copies:
        copy.wait()


def scatter_rows(parts, rows, bases, row_count, bias=None):
    last = bias is not None
    vmem = pl.BlockSpec(memory_space=pltpu.VMEM)
    return pl.pallas_call(
        functools.partial(scatter_kernel, blocks=len(parts), bases=len(bases), last=last),
        in_specs=[pl.BlockSpec(memory_space=pltpu.SMEM)] + [vmem] * (len(parts) + len(bases) + last),
        out_specs=pl.BlockSpec(memory_space=pltpu.HBM) if last else vmem,
        out_shape=jax.ShapeDtypeStruct((HALF, row_count), jnp.float32),
        scratch_shapes=[pltpu.VMEM((row_count + 8, LANES), jnp.float32)] * 4
        + ([pltpu.VMEM((HALF, row_count), jnp.float32), pltpu.SemaphoreType.DMA((8,))] if last else []),
        compiler_params=pltpu.CompilerParams(vmem_limit_bytes=13 * 2**20),
        cost_estimate=pl.CostEstimate(flops=10**7, bytes_accessed=16 * 2**20, transcendentals=0),
    )(rows, *parts, *bases, *([bias] if last else []))


def shifted(value, count, step):
    return lax.ppermute(value, "feat", [(i, (i + step) % count) for i in range(count)])


def per_device(
    features,
    w_self,
    w_neigh,
    out_bias,
    hub_rows,
    replica_send_rows,
    ret_rows,
    tile_src,
    tile_dst,
    tile_vals,
    *,
    feat,
):
    xt = features.T
    peers, slot = replica_send_rows.shape[1:]
    ret = ret_rows.shape[2]
    outgoing = gather_rows(xt, replica_send_rows[0], hub_rows[0])
    mirror = lax.all_to_all(outgoing, "dom", split_axis=0, concat_axis=0, tiled=True)

    me = lax.axis_index("feat")
    width = xt.shape[0]
    neighbours = [w_neigh] + [shifted(w_neigh, feat, -d) for d in range(1, feat)]
    xt, tiles, neighbours = lax.optimization_barrier((xt, tile_vals[0], neighbours))
    blocks = [xt] + [shifted(xt, feat, d) for d in range(1, feat)]
    split_vals, tile_order = split_tiles(tiles, tile_src[0], tile_dst[0])

    mirror, split_vals, tile_order = lax.optimization_barrier((mirror, split_vals, tile_order))
    rows = slot // 2
    hub_count = hub_rows.shape[1] * peers // slot
    hub_half = mirror[:, rows:]
    hub_other = lax.ppermute(hub_half, "dom", [(i, i ^ 1) for i in range(peers)])
    side = (lax.axis_index("dom") % 2).astype(jnp.int32).reshape(1)
    partial, hub_vals = listed_tiles(split_vals, mirror, tile_order, rows, hub_count, peers * ret // slot)
    partial = hub_tiles(hub_vals, hub_half, hub_other, partial, tile_order, side)
    partial, blocks, neighbours, w_self, ret_rows = lax.optimization_barrier(
        (partial, blocks, neighbours, w_self, ret_rows)
    )
    slots = lax.all_to_all(partial, ("dom", "feat"), split_axis=0, concat_axis=0, tiled=True)

    self_rows = w_self.reshape(feat, width, -1)
    self_rows = jnp.concatenate(
        [lax.dynamic_index_in_dim(self_rows, (me - d) % feat, 0, False) for d in range(feat)]
    )
    own = lax.dot_general(
        self_rows,
        jnp.concatenate(blocks),
        (((0,), (0,)), ((), ())),
        precision=lax.Precision.HIGHEST,
        preferred_element_type=jnp.float32,
    )
    weights = []
    for mine in neighbours:
        mine = mine.reshape(feat, width, width)
        empty = jnp.zeros_like(mine)
        weights.append(
            jnp.stack([jnp.concatenate([mine, empty], 2), jnp.concatenate([empty, mine], 2)], 1).reshape(
                feat * LANES, LANES
            )
        )
    weights = split_weights(jnp.stack(weights))
    quarters = ret_rows[0].reshape(peers, feat, 2, 8).transpose(1, 0, 3, 2)
    order = [
        lax.dynamic_index_in_dim(quarters, (me - d) % feat, 0, False).reshape(-1) for d in range(feat)
    ]
    far = feat // 2
    near = [d for d in range(feat - 1, 0, -1) if d != far]
    near_rows = jnp.concatenate([order[d] for d in near])
    bias = out_bias[:, None]
    row_count = features.shape[0]
    slots, own, weights, near_rows, order, bias = lax.optimization_barrier(
        (slots, own, weights, near_rows, order, bias)
    )
    slots = slots.reshape(peers, feat, 8, LANES)
    targets = (far, *near)
    kept, *parts = project_slots(slots, weights, targets)
    moved = {d: shifted(part, feat, d) for d, part in zip(targets, parts)}
    total = scatter_rows([kept], order[0], [own], row_count)
    total = scatter_rows([moved[far]], order[far], [total], row_count)
    return scatter_rows([moved[d] for d in near], near_rows, [total], row_count, bias).T


def solution(mesh):
    return jax.shard_map(
        functools.partial(per_device, feat=mesh.shape["feat"]),
        mesh=mesh,
        in_specs=(
            P("dom", "feat"),
            P(None, "feat"),
            P(None, "feat"),
            P("feat"),
            P("dom", None),
            P("dom", None, None),
            P("dom", None, None),
            P("dom", None),
            P("dom", None),
            P("dom", None, None, None),
        ),
        out_specs=P("dom", "feat"),
        check_vma=False,
    )
```

```python
import functools

import jax
import jax.numpy as jnp
from jax import lax
from jax.experimental import pallas as pl
from jax.experimental.pallas import tpu as pltpu
from jax.sharding import PartitionSpec as P

LANES = 128
KERNEL_VMEM = 46 * 2**20
HALF = 64


def left_half(shape):
    return lax.broadcasted_iota(jnp.int32, shape, len(shape) - 1) < HALF


def gather_kernel(
    rows_hbm, hubs_hbm, xt_hbm, out_hbm, rows_ref, hubs_ref, xt_ref, table_ref, hub_ref, out_ref, sems, list_sems, out_sems,
    *, rows, hub_rows
):
    lists = [
        pltpu.make_async_copy(rows_hbm, rows_ref, list_sems.at[0]),
        pltpu.make_async_copy(hubs_hbm, hubs_ref, list_sems.at[1]),
    ]
    for copy in lists:
        copy.start()
    chunks = sems.shape[0]
    width = xt_ref.shape[1] // chunks

    def fetch(c):
        columns = pl.ds(c * width, width)
        return pltpu.make_async_copy(xt_hbm.at[:, columns], xt_ref.at[:, columns], sems.at[c])

    for c in range(chunks):
        fetch(c).start()
    for c in range(chunks):
        fetch(c).wait()
        part = xt_ref[:, c * width : (c + 1) * width]
        table_ref[c * width : (c + 1) * width, :] = jnp.concatenate([part, part], axis=0).T
    for copy in lists:
        copy.wait()

    left = left_half((1, LANES))

    def pick(first, second):
        return jnp.where(left, table_ref[pl.ds(first, 1), :], table_ref[pl.ds(second, 1), :])

    for half in range(2):
        start = half * 2 * hub_rows
        for i in range(hub_rows):
            hub_ref[half, i : i + 1, :] = pick(hubs_ref[start + i], hubs_ref[start + hub_rows + i])

    def one(peer, carry):
        base = peer * 2 * rows
        for i in range(rows):
            out_ref[peer, i : i + 1, :] = pick(rows_ref[base + i], rows_ref[base + rows + i])
        out_ref[peer, rows : rows + hub_rows, :] = hub_ref[lax.rem(peer, 2)]
        return carry

    groups = out_sems.shape[0]
    peers = out_ref.shape[0] // groups

    def send(g):
        span = pl.ds(g * peers, peers)
        return pltpu.make_async_copy(out_ref.at[span], out_hbm.at[span], out_sems.at[g])

    def group(g, carry):
        lax.fori_loop(g * peers, (g + 1) * peers, one, 0)
        send(g).start()
        return carry

    lax.fori_loop(0, groups, group, 0)
    for g in range(groups):
        send(g).wait()


def gather_rows(xt, send_rows, hub_list):
    peer_count = send_rows.shape[0]
    rows = send_rows.shape[1] // 2
    hub_rows = hub_list.shape[0] // 4
    shape = (peer_count, rows + hub_rows, LANES)
    return pl.pallas_call(
        functools.partial(gather_kernel, rows=rows, hub_rows=hub_rows),
        in_specs=[pl.BlockSpec(memory_space=pltpu.HBM)] * 3,
        out_specs=pl.BlockSpec(memory_space=pltpu.HBM),
        scratch_shapes=[
            pltpu.SMEM((send_rows.size,), jnp.int32),
            pltpu.SMEM(hub_list.shape, jnp.int32),
            pltpu.VMEM(xt.shape, jnp.float32),
            pltpu.VMEM((xt.shape[1], LANES), jnp.float32),
            pltpu.VMEM((2, hub_rows, LANES), jnp.float32),
            pltpu.VMEM(shape, jnp.float32),
            pltpu.SemaphoreType.DMA((8,)),
            pltpu.SemaphoreType.DMA((2,)),
            pltpu.SemaphoreType.DMA((16,)),
        ],
        out_shape=jax.ShapeDtypeStruct(shape, jnp.float32),
        compiler_params=pltpu.CompilerParams(vmem_limit_bytes=60 * 2**20),
        cost_estimate=pl.CostEstimate(flops=10**7, bytes_accessed=4 * 2**20, transcendentals=0),
    )(send_rows.reshape(-1), hub_list, xt)


def split(value):
    high = value.astype(jnp.bfloat16)
    mid = (value - high.astype(jnp.float32)).astype(jnp.bfloat16)
    return high, mid


def split_kernel(src_ref, dst_ref, tiles_ref, out_ref, order_ref):
    count = tiles_ref.shape[0]
    for i in range(count):
        tile = pl.program_id(0) * count + i
        source = src_ref[tile]
        high, mid = split(tiles_ref[i])
        out_ref[source, :, :LANES] = high
        out_ref[source, :, LANES:] = mid
        order_ref[source] = dst_ref[tile]


def split_tiles(tile_vals, tile_src, tile_dst):
    tiles, size, _ = tile_vals.shape
    step = 8
    return pl.pallas_call(
        split_kernel,
        grid_spec=pltpu.PrefetchScalarGridSpec(
            num_scalar_prefetch=2,
            grid=(tiles // step,),
            in_specs=[pl.BlockSpec((step, size, size), lambda i, *_: (i, 0, 0))],
            out_specs=[
                pl.BlockSpec((tiles, size, 2 * size), lambda i, *_: (0, 0, 0)),
                pl.BlockSpec(memory_space=pltpu.SMEM),
            ],
        ),
        out_shape=[
            jax.ShapeDtypeStruct((tiles, size, 2 * size), jnp.bfloat16),
            jax.ShapeDtypeStruct((tiles,), jnp.int32),
        ],
        compiler_params=pltpu.CompilerParams(vmem_limit_bytes=40 * 2**20),
        cost_estimate=pl.CostEstimate(flops=10**7, bytes_accessed=12 * 2**20, transcendentals=0),
    )(tile_src, tile_dst, tile_vals)


def unpack(packed):
    left = left_half(packed.shape)
    swapped = pltpu.roll(packed, HALF, 1)
    return jnp.where(left, packed, swapped), jnp.where(left, swapped, packed)


def multiply(tile, block):
    top, mid = split(block)
    right_side = jnp.concatenate(
        [jnp.concatenate([top, mid], axis=1), jnp.concatenate([mid, top], axis=1)], axis=0
    )
    product = jnp.dot(tile, right_side, preferred_element_type=jnp.float32)
    return product[:, :LANES] + product[:, LANES:]


def packed_sums(acc_ref, block, part):
    first = acc_ref[block, part * 16 : part * 16 + 8, :]
    second = acc_ref[block, part * 16 + 8 : part * 16 + 16, :]
    return jnp.where(left_half((8, LANES)), first, second)


def listed_kernel(
    dst_hbm, tiles_hbm, mirror_ref, acc_ref, hub_tiles_ref, dst_ref, tiles_ref, sems, hub_sem, dst_sem, *, first, rows
):
    places = pltpu.make_async_copy(dst_hbm, dst_ref, dst_sem)
    places.start()
    chunks = sems.shape[0]
    count = tiles_ref.shape[0] // chunks

    def fetch(c):
        return pltpu.make_async_copy(
            tiles_hbm.at[pl.ds(first + c * count, count)], tiles_ref.at[pl.ds(c * count, count)], sems.at[c]
        )

    piece = count // 4
    for c in range(chunks * 4):
        pltpu.make_async_copy(
            tiles_hbm.at[pl.ds(first + c * piece, piece)], tiles_ref.at[pl.ds(c * piece, piece)], sems.at[c // 4]
        ).start()
    hubs = pltpu.make_async_copy(tiles_hbm.at[pl.ds(0, first)], hub_tiles_ref, hub_sem)
    acc_ref[...] = jnp.zeros_like(acc_ref)
    places.wait()

    def chunk(c, carry):
        fetch(c).wait()

        @pl.when(c == 1)
        def _():
            hubs.start()

        for i in range(count):
            tile = c * count + i
            low, high = unpack(mirror_ref[tile, :rows, :])
            acc_ref[dst_ref[first + tile]] += multiply(tiles_ref[tile], jnp.concatenate([low, high], axis=0))
        return carry

    lax.fori_loop(0, chunks, chunk, 0)
    hubs.wait()


def listed_tiles(split_vals, mirror, order, rows, first, dst_blocks):
    tiles, size, _ = split_vals.shape
    count = tiles - first
    whole = pl.BlockSpec(memory_space=pltpu.VMEM)
    return pl.pallas_call(
        functools.partial(listed_kernel, first=first, rows=rows),
        in_specs=[pl.BlockSpec(memory_space=pltpu.HBM), pl.BlockSpec(memory_space=pltpu.HBM), whole],
        out_specs=[whole, whole],
        scratch_shapes=[
            pltpu.SMEM(order.shape, jnp.int32),
            pltpu.VMEM((count, size, 2 * size), jnp.bfloat16),
            pltpu.SemaphoreType.DMA((8,)),
            pltpu.SemaphoreType.DMA,
            pltpu.SemaphoreType.DMA,
        ],
        out_shape=[
            jax.ShapeDtypeStruct((dst_blocks, size, LANES), jnp.float32),
            jax.ShapeDtypeStruct((first, size, 2 * size), jnp.bfloat16),
        ],
        compiler_params=pltpu.CompilerParams(vmem_limit_bytes=KERNEL_VMEM),
        cost_estimate=pl.CostEstimate(flops=10**9, bytes_accessed=10 * 2**20, transcendentals=0),
    )(order, split_vals, mirror)


def hub_kernel(
    dst_hbm, tiles_ref, own_ref, other_ref, before_ref, out_hbm, dst_ref, hubs_ref, acc_ref, out_ref, out_sems, dst_sem
):
    places = pltpu.make_async_copy(dst_hbm, dst_ref, dst_sem)
    places.start()
    count = 8
    chunks = tiles_ref.shape[0] // count
    acc_ref[...] = before_ref[...]
    places.wait()
    side = dst_ref[dst_ref.shape[0] - 1]
    hubs_ref[side] = own_ref[...]
    hubs_ref[1 - side] = other_ref[...]

    def chunk(c, carry):
        for i in range(count):
            tile = c * count + i
            pieces = []
            for part in range(2):
                for half in range(2):
                    pieces.extend(unpack(hubs_ref[half, 2 * tile + part]))
            acc_ref[dst_ref[tile]] += multiply(tiles_ref[tile], jnp.concatenate(pieces, axis=0))
        return carry

    lax.fori_loop(0, chunks, chunk, 0)
    sends = out_sems.shape[0]
    blocks = acc_ref.shape[0] // sends
    results = []
    for c in range(sends):
        for block in range(c * blocks, (c + 1) * blocks):
            for part in range(8):
                out_ref[block * 8 + part] = packed_sums(acc_ref, block, part)
        span = pl.ds(c * blocks * 8, blocks * 8)
        results.append(pltpu.make_async_copy(out_ref.at[span], out_hbm.at[span], out_sems.at[c]))
        results[-1].start()
    for copy in results:
        copy.wait()


def hub_tiles(split_vals, own, other, before, order):
    blocks, size, _ = before.shape
    result = jax.ShapeDtypeStruct((blocks * 8, 8, LANES), jnp.float32)
    return pl.pallas_call(
        hub_kernel,
        in_specs=[pl.BlockSpec(memory_space=pltpu.HBM)] + [pl.BlockSpec(memory_space=pltpu.VMEM)] * 4,
        out_specs=pl.BlockSpec(memory_space=pltpu.HBM),
        scratch_shapes=[
            pltpu.SMEM(order.shape, jnp.int32),
            pltpu.VMEM((2,) + own.shape, jnp.float32),
            pltpu.VMEM(before.shape, jnp.float32),
            pltpu.VMEM(result.shape, jnp.float32),
            pltpu.SemaphoreType.DMA((4,)),
            pltpu.SemaphoreType.DMA,
        ],
        out_shape=result,
        compiler_params=pltpu.CompilerParams(vmem_limit_bytes=KERNEL_VMEM),
        cost_estimate=pl.CostEstimate(flops=10**9, bytes_accessed=6 * 2**20, transcendentals=0),
    )(order, split_vals, own, other, before)


def weights_kernel(weights_ref, out_ref):
    for d in range(weights_ref.shape[0]):
        top, mid = split(weights_ref[d])
        depth = top.shape[0]
        out_ref[d, :depth, :LANES] = top
        out_ref[d, :depth, LANES:] = mid
        out_ref[d, depth:, :LANES] = mid
        out_ref[d, depth:, LANES:] = top


def split_weights(weights):
    count, depth, width = weights.shape
    return pl.pallas_call(
        weights_kernel,
        out_shape=jax.ShapeDtypeStruct((count, 2 * depth, 2 * width), jnp.bfloat16),
    )(weights)


def slots_kernel(slots_ref, weights_ref, kept_ref, *refs, targets):
    moved = len(targets)
    out_refs, (held_ref, sems) = refs[:moved], refs[moved:]
    peers = slots_ref.shape[0]
    blocks = slots_ref.shape[1]
    tops, mids = [], []
    for k in range(blocks):
        top, mid = split(slots_ref[:, k].reshape(peers * 8, LANES))
        tops.append(top)
        mids.append(mid)
    whole = jnp.concatenate(tops + mids, axis=1)

    def product(d):
        both = jnp.dot(whole, weights_ref[d], preferred_element_type=jnp.float32)
        return both[:, :LANES] + both[:, LANES:]

    copies = []
    for i, d in enumerate(targets):
        held_ref[i] = product(d)
        copies.append(pltpu.make_async_copy(held_ref.at[i], out_refs[i], sems.at[i]))
        copies[-1].start()
    kept_ref[...] = product(0)
    for copy in copies:
        copy.wait()


def project_slots(slots, weights, targets):
    peers = slots.shape[0]
    moved = len(targets)
    shape = jax.ShapeDtypeStruct((peers * 8, LANES), jnp.float32)
    vmem = pl.BlockSpec(memory_space=pltpu.VMEM)
    return pl.pallas_call(
        functools.partial(slots_kernel, targets=targets),
        in_specs=[vmem, vmem],
        out_specs=[vmem] + [pl.BlockSpec(memory_space=pltpu.HBM)] * moved,
        out_shape=[shape] * (moved + 1),
        scratch_shapes=[
            pltpu.VMEM((moved,) + shape.shape, jnp.float32),
            pltpu.SemaphoreType.DMA((moved,)),
        ],
        compiler_params=pltpu.CompilerParams(vmem_limit_bytes=12 * 2**20),
        cost_estimate=pl.CostEstimate(flops=10**7, bytes_accessed=4 * 2**20, transcendentals=0),
    )(slots, weights)


def scatter_kernel(rows_hbm, *refs, blocks, bases, last):
    *refs, rows_ref, rows_sem = refs
    lists = pltpu.make_async_copy(rows_hbm, rows_ref, rows_sem)
    lists.start()
    parts = refs[:blocks]
    base_refs = refs[blocks : blocks + bases]
    bias_ref = refs[blocks + bases] if last else None
    refs = refs[blocks + bases + last :]
    if last:
        out_hbm, *sums, out_ref, sems = refs
    else:
        out_ref, *sums = refs
    for total in sums:
        total[...] = jnp.zeros_like(total)
    lists.wait()
    left = left_half((1, LANES))
    zero = jnp.zeros((1, LANES), jnp.float32)
    lanes = len(sums) // 2
    for d, part in enumerate(parts):
        count = part.shape[0]

        def add(g, carry, part=part, d=d, count=count):
            for i in range(lanes):
                row = g * lanes + i
                value = part[pl.ds(row, 1), :]
                first = rows_ref[(d * count + row) * 2]
                second = rows_ref[(d * count + row) * 2 + 1]
                sums[2 * i][pl.ds(first, 1), :] += jnp.where(left, value, zero)
                sums[2 * i + 1][pl.ds(second, 1), :] += jnp.where(left, zero, value)
            return carry

        lax.fori_loop(0, count // lanes, add, 0, unroll=8)
    width = 512
    copies = []
    for c in range(out_ref.shape[1] // width):
        columns = slice(c * width, (c + 1) * width)
        whole = functools.reduce(lambda a, b: a + b, [total[columns, :] for total in sums])
        turned = whole.T
        result = turned[:HALF] + turned[HALF:]
        for base in base_refs:
            result = result + base[:, columns]
        out_ref[:, columns] = jnp.maximum(result + bias_ref[...], 0.0) if last else result
        if last:
            copies.append(pltpu.make_async_copy(out_ref.at[:, columns], out_hbm.at[:, columns], sems.at[c]))
            copies[-1].start()
    for copy in copies:
        copy.wait()


def scatter_rows(parts, rows, bases, row_count, bias=None):
    last = bias is not None
    vmem = pl.BlockSpec(memory_space=pltpu.VMEM)
    return pl.pallas_call(
        functools.partial(scatter_kernel, blocks=len(parts), bases=len(bases), last=last),
        in_specs=[pl.BlockSpec(memory_space=pltpu.HBM)] + [vmem] * (len(parts) + len(bases) + last),
        out_specs=pl.BlockSpec(memory_space=pltpu.HBM) if last else vmem,
        out_shape=jax.ShapeDtypeStruct((HALF, row_count), jnp.float32),
        scratch_shapes=[pltpu.VMEM((row_count + 8, LANES), jnp.float32)] * 4
        + ([pltpu.VMEM((HALF, row_count), jnp.float32), pltpu.SemaphoreType.DMA((8,))] if last else [])
        + [pltpu.SMEM(rows.shape, jnp.int32), pltpu.SemaphoreType.DMA],
        compiler_params=pltpu.CompilerParams(vmem_limit_bytes=13 * 2**20),
        cost_estimate=pl.CostEstimate(flops=10**7, bytes_accessed=16 * 2**20, transcendentals=0),
    )(rows, *parts, *bases, *([bias] if last else []))


def shifted(value, count, step):
    return lax.ppermute(value, "feat", [(i, (i + step) % count) for i in range(count)])


def per_device(
    features,
    w_self,
    w_neigh,
    out_bias,
    hub_rows,
    replica_send_rows,
    ret_rows,
    tile_src,
    tile_dst,
    tile_vals,
    *,
    feat,
):
    xt = features.T
    peers, slot = replica_send_rows.shape[1:]
    ret = ret_rows.shape[2]
    outgoing = gather_rows(xt, replica_send_rows[0], hub_rows[0])
    mirror = lax.all_to_all(outgoing, "dom", split_axis=0, concat_axis=0, tiled=True)

    me = lax.axis_index("feat")
    width = xt.shape[0]
    neighbours = [w_neigh] + [shifted(w_neigh, feat, -d) for d in range(1, feat)]
    xt, tiles, neighbours = lax.optimization_barrier((xt, tile_vals[0], neighbours))
    blocks = [xt] + [shifted(xt, feat, d) for d in range(1, feat)]
    split_vals, tile_order = split_tiles(tiles, tile_src[0], tile_dst[0])

    side = (lax.axis_index("dom") % 2).astype(jnp.int32).reshape(1)
    tile_order = jnp.concatenate([tile_order, jnp.zeros((31,), jnp.int32), side])
    mirror, split_vals, tile_order = lax.optimization_barrier((mirror, split_vals, tile_order))
    rows = slot // 2
    hub_count = hub_rows.shape[1] * peers // slot
    hub_half = mirror[:, rows:]
    hub_other = lax.ppermute(hub_half, "dom", [(i, i ^ 1) for i in range(peers)])
    partial, hub_vals = listed_tiles(split_vals, mirror, tile_order, rows, hub_count, peers * ret // slot)
    partial = hub_tiles(hub_vals, hub_half, hub_other, partial, tile_order)
    partial, blocks, neighbours, w_self, ret_rows = lax.optimization_barrier(
        (partial, blocks, neighbours, w_self, ret_rows)
    )
    slots = lax.all_to_all(partial, ("dom", "feat"), split_axis=0, concat_axis=0, tiled=True)

    self_rows = w_self.reshape(feat, width, -1)
    self_rows = jnp.concatenate(
        [lax.dynamic_index_in_dim(self_rows, (me - d) % feat, 0, False) for d in range(feat)]
    )
    own = lax.dot_general(
        self_rows,
        jnp.concatenate(blocks),
        (((0,), (0,)), ((), ())),
        precision=lax.Precision.HIGHEST,
        preferred_element_type=jnp.float32,
    )
    weights = []
    for mine in neighbours:
        mine = mine.reshape(feat, width, width)
        empty = jnp.zeros_like(mine)
        weights.append(
            jnp.stack([jnp.concatenate([mine, empty], 2), jnp.concatenate([empty, mine], 2)], 1).reshape(
                feat * LANES, LANES
            )
        )
    weights = split_weights(jnp.stack(weights))
    quarters = ret_rows[0].reshape(peers, feat, 2, 8).transpose(1, 0, 3, 2)
    order = [
        lax.dynamic_index_in_dim(quarters, (me - d) % feat, 0, False).reshape(-1) for d in range(feat)
    ]
    far = feat // 2
    near = [d for d in range(feat - 1, 0, -1) if d != far]
    near_rows = jnp.concatenate([order[d] for d in near])
    bias = out_bias[:, None]
    row_count = features.shape[0]
    slots, own, weights, near_rows, order, bias = lax.optimization_barrier(
        (slots, own, weights, near_rows, order, bias)
    )
    slots = slots.reshape(peers, feat, 8, LANES)
    targets = (far, *near)
    kept, *parts = project_slots(slots, weights, targets)
    moved = {d: shifted(part, feat, d) for d, part in zip(targets, parts)}
    total = scatter_rows([kept], order[0], [own], row_count)
    total = scatter_rows([moved[far]], order[far], [total], row_count)
    return scatter_rows([moved[d] for d in near], near_rows, [total], row_count, bias).T


def solution(mesh):
    return jax.shard_map(
        functools.partial(per_device, feat=mesh.shape["feat"]),
        mesh=mesh,
        in_specs=(
            P("dom", "feat"),
            P(None, "feat"),
            P(None, "feat"),
            P("feat"),
            P("dom", None),
            P("dom", None, None),
            P("dom", None, None),
            P("dom", None),
            P("dom", None),
            P("dom", None, None, None),
        ),
        out_specs=P("dom", "feat"),
        check_vma=False,
    )
```

```python
import functools

import jax
import jax.numpy as jnp
from jax import lax
from jax.experimental import pallas as pl
from jax.experimental.pallas import tpu as pltpu
from jax.sharding import PartitionSpec as P

LANES = 128
KERNEL_VMEM = 46 * 2**20
HALF = 64


def left_half(shape):
    return lax.broadcasted_iota(jnp.int32, shape, len(shape) - 1) < HALF


def gather_kernel(
    rows_hbm, hubs_hbm, xt_hbm, out_hbm, rows_ref, hubs_ref, xt_ref, table_ref, hub_ref, out_ref, sems, list_sems, out_sems,
    *, rows, hub_rows
):
    lists = [
        pltpu.make_async_copy(rows_hbm, rows_ref, list_sems.at[0]),
        pltpu.make_async_copy(hubs_hbm, hubs_ref, list_sems.at[1]),
    ]
    for copy in lists:
        copy.start()
    chunks = sems.shape[0]
    width = xt_ref.shape[1] // chunks

    def fetch(c):
        columns = pl.ds(c * width, width)
        return pltpu.make_async_copy(xt_hbm.at[:, columns], xt_ref.at[:, columns], sems.at[c])

    for c in range(chunks):
        fetch(c).start()
    for c in range(chunks):
        fetch(c).wait()
        part = xt_ref[:, c * width : (c + 1) * width]
        table_ref[c * width : (c + 1) * width, :] = jnp.concatenate([part, part], axis=0).T
    for copy in lists:
        copy.wait()

    left = left_half((1, LANES))

    def pick(first, second):
        return jnp.where(left, table_ref[pl.ds(first, 1), :], table_ref[pl.ds(second, 1), :])

    for half in range(2):
        start = half * 2 * hub_rows
        for i in range(hub_rows):
            hub_ref[half, i : i + 1, :] = pick(hubs_ref[start + i], hubs_ref[start + hub_rows + i])

    def one(peer, carry):
        base = peer * 2 * rows
        for i in range(rows):
            out_ref[peer, i : i + 1, :] = pick(rows_ref[base + i], rows_ref[base + rows + i])
        out_ref[peer, rows : rows + hub_rows, :] = hub_ref[lax.rem(peer, 2)]
        return carry

    groups = out_sems.shape[0]
    peers = out_ref.shape[0] // groups

    def send(g):
        span = pl.ds(g * peers, peers)
        return pltpu.make_async_copy(out_ref.at[span], out_hbm.at[span], out_sems.at[g])

    def group(g, carry):
        lax.fori_loop(g * peers, (g + 1) * peers, one, 0)
        send(g).start()
        return carry

    lax.fori_loop(0, groups, group, 0)
    for g in range(groups):
        send(g).wait()


def gather_rows(xt, send_rows, hub_list):
    peer_count = send_rows.shape[0]
    rows = send_rows.shape[1] // 2
    hub_rows = hub_list.shape[0] // 4
    shape = (peer_count, rows + hub_rows, LANES)
    return pl.pallas_call(
        functools.partial(gather_kernel, rows=rows, hub_rows=hub_rows),
        in_specs=[pl.BlockSpec(memory_space=pltpu.HBM)] * 3,
        out_specs=pl.BlockSpec(memory_space=pltpu.HBM),
        scratch_shapes=[
            pltpu.SMEM((send_rows.size,), jnp.int32),
            pltpu.SMEM(hub_list.shape, jnp.int32),
            pltpu.VMEM(xt.shape, jnp.float32),
            pltpu.VMEM((xt.shape[1], LANES), jnp.float32),
            pltpu.VMEM((2, hub_rows, LANES), jnp.float32),
            pltpu.VMEM(shape, jnp.float32),
            pltpu.SemaphoreType.DMA((8,)),
            pltpu.SemaphoreType.DMA((2,)),
            pltpu.SemaphoreType.DMA((16,)),
        ],
        out_shape=jax.ShapeDtypeStruct(shape, jnp.float32),
        compiler_params=pltpu.CompilerParams(vmem_limit_bytes=60 * 2**20),
        cost_estimate=pl.CostEstimate(flops=10**7, bytes_accessed=4 * 2**20, transcendentals=0),
    )(send_rows.reshape(-1), hub_list, xt)


def split(value):
    high = value.astype(jnp.bfloat16)
    mid = (value - high.astype(jnp.float32)).astype(jnp.bfloat16)
    return high, mid


def split_kernel(src_ref, dst_ref, tiles_ref, out_ref, order_ref):
    count = tiles_ref.shape[0]
    for i in range(count):
        tile = pl.program_id(0) * count + i
        source = src_ref[tile]
        high, mid = split(tiles_ref[i])
        out_ref[source, :, :LANES] = high
        out_ref[source, :, LANES:] = mid
        order_ref[source] = dst_ref[tile]


def split_tiles(tile_vals, tile_src, tile_dst):
    tiles, size, _ = tile_vals.shape
    step = 8
    return pl.pallas_call(
        split_kernel,
        grid_spec=pltpu.PrefetchScalarGridSpec(
            num_scalar_prefetch=2,
            grid=(tiles // step,),
            in_specs=[pl.BlockSpec((step, size, size), lambda i, *_: (i, 0, 0))],
            out_specs=[
                pl.BlockSpec((tiles, size, 2 * size), lambda i, *_: (0, 0, 0)),
                pl.BlockSpec(memory_space=pltpu.SMEM),
            ],
        ),
        out_shape=[
            jax.ShapeDtypeStruct((tiles, size, 2 * size), jnp.bfloat16),
            jax.ShapeDtypeStruct((tiles,), jnp.int32),
        ],
        compiler_params=pltpu.CompilerParams(vmem_limit_bytes=40 * 2**20),
        cost_estimate=pl.CostEstimate(flops=10**7, bytes_accessed=12 * 2**20, transcendentals=0),
    )(tile_src, tile_dst, tile_vals)


def unpack(packed):
    left = left_half(packed.shape)
    swapped = pltpu.roll(packed, HALF, 1)
    return jnp.where(left, packed, swapped), jnp.where(left, swapped, packed)


def multiply(tile, block):
    top, mid = split(block)
    right_side = jnp.concatenate(
        [jnp.concatenate([top, mid], axis=1), jnp.concatenate([mid, top], axis=1)], axis=0
    )
    product = jnp.dot(tile, right_side, preferred_element_type=jnp.float32)
    return product[:, :LANES] + product[:, LANES:]


def packed_sums(acc_ref, block, part):
    first = acc_ref[block, part * 16 : part * 16 + 8, :]
    second = acc_ref[block, part * 16 + 8 : part * 16 + 16, :]
    return jnp.where(left_half((8, LANES)), first, second)


def listed_kernel(
    dst_hbm, tiles_hbm, mirror_ref, acc_ref, hub_tiles_ref, dst_ref, tiles_ref, sems, hub_sem, dst_sem, *, first, rows
):
    places = pltpu.make_async_copy(dst_hbm, dst_ref, dst_sem)
    places.start()
    chunks = sems.shape[0]
    count = tiles_ref.shape[0] // chunks

    def fetch(c):
        return pltpu.make_async_copy(
            tiles_hbm.at[pl.ds(first + c * count, count)], tiles_ref.at[pl.ds(c * count, count)], sems.at[c]
        )

    piece = count // 4
    for c in range(chunks * 4):
        pltpu.make_async_copy(
            tiles_hbm.at[pl.ds(first + c * piece, piece)], tiles_ref.at[pl.ds(c * piece, piece)], sems.at[c // 4]
        ).start()
    hubs = pltpu.make_async_copy(tiles_hbm.at[pl.ds(0, first)], hub_tiles_ref, hub_sem)
    acc_ref[...] = jnp.zeros_like(acc_ref)
    places.wait()

    def chunk(c, carry):
        fetch(c).wait()

        @pl.when(c == 1)
        def _():
            hubs.start()

        for i in range(count):
            tile = c * count + i
            low, high = unpack(mirror_ref[tile, :rows, :])
            acc_ref[dst_ref[first + tile]] += multiply(tiles_ref[tile], jnp.concatenate([low, high], axis=0))
        return carry

    lax.fori_loop(0, chunks, chunk, 0)
    hubs.wait()


def listed_tiles(split_vals, mirror, order, rows, first, dst_blocks):
    tiles, size, _ = split_vals.shape
    count = tiles - first
    whole = pl.BlockSpec(memory_space=pltpu.VMEM)
    return pl.pallas_call(
        functools.partial(listed_kernel, first=first, rows=rows),
        in_specs=[pl.BlockSpec(memory_space=pltpu.HBM), pl.BlockSpec(memory_space=pltpu.HBM), whole],
        out_specs=[whole, whole],
        scratch_shapes=[
            pltpu.SMEM(order.shape, jnp.int32),
            pltpu.VMEM((count, size, 2 * size), jnp.bfloat16),
            pltpu.SemaphoreType.DMA((8,)),
            pltpu.SemaphoreType.DMA,
            pltpu.SemaphoreType.DMA,
        ],
        out_shape=[
            jax.ShapeDtypeStruct((dst_blocks, size, LANES), jnp.float32),
            jax.ShapeDtypeStruct((first, size, 2 * size), jnp.bfloat16),
        ],
        compiler_params=pltpu.CompilerParams(vmem_limit_bytes=KERNEL_VMEM),
        cost_estimate=pl.CostEstimate(flops=10**9, bytes_accessed=10 * 2**20, transcendentals=0),
    )(order, split_vals, mirror)


def hub_kernel(
    dst_hbm, tiles_ref, own_ref, other_ref, before_ref, out_hbm, dst_ref, acc_ref, out_ref, out_sems, dst_sem
):
    places = pltpu.make_async_copy(dst_hbm, dst_ref, dst_sem)
    places.start()
    count = 8
    chunks = tiles_ref.shape[0] // count
    acc_ref[...] = before_ref[...]
    places.wait()
    first = dst_ref[dst_ref.shape[0] - 1] == 0

    def chunk(c, carry):
        for i in range(count):
            tile = c * count + i
            pieces = []
            for part in range(2):
                own, other = own_ref[2 * tile + part], other_ref[2 * tile + part]
                pieces.extend(unpack(jnp.where(first, own, other)))
                pieces.extend(unpack(jnp.where(first, other, own)))
            acc_ref[dst_ref[tile]] += multiply(tiles_ref[tile], jnp.concatenate(pieces, axis=0))
        return carry

    lax.fori_loop(0, chunks, chunk, 0)
    sends = out_sems.shape[0]
    blocks = acc_ref.shape[0] // sends
    results = []
    for c in range(sends):
        for block in range(c * blocks, (c + 1) * blocks):
            for part in range(8):
                out_ref[block * 8 + part] = packed_sums(acc_ref, block, part)
        span = pl.ds(c * blocks * 8, blocks * 8)
        results.append(pltpu.make_async_copy(out_ref.at[span], out_hbm.at[span], out_sems.at[c]))
        results[-1].start()
    for copy in results:
        copy.wait()


def hub_tiles(split_vals, own, other, before, order):
    blocks, size, _ = before.shape
    result = jax.ShapeDtypeStruct((blocks * 8, 8, LANES), jnp.float32)
    return pl.pallas_call(
        hub_kernel,
        in_specs=[pl.BlockSpec(memory_space=pltpu.HBM)] + [pl.BlockSpec(memory_space=pltpu.VMEM)] * 4,
        out_specs=pl.BlockSpec(memory_space=pltpu.HBM),
        scratch_shapes=[
            pltpu.SMEM(order.shape, jnp.int32),
            pltpu.VMEM(before.shape, jnp.float32),
            pltpu.VMEM(result.shape, jnp.float32),
            pltpu.SemaphoreType.DMA((8,)),
            pltpu.SemaphoreType.DMA,
        ],
        out_shape=result,
        compiler_params=pltpu.CompilerParams(vmem_limit_bytes=KERNEL_VMEM),
        cost_estimate=pl.CostEstimate(flops=10**9, bytes_accessed=6 * 2**20, transcendentals=0),
    )(order, split_vals, own, other, before)


def weights_kernel(weights_ref, out_ref):
    for d in range(weights_ref.shape[0]):
        top, mid = split(weights_ref[d])
        depth = top.shape[0]
        out_ref[d, :depth, :LANES] = top
        out_ref[d, :depth, LANES:] = mid
        out_ref[d, depth:, :LANES] = mid
        out_ref[d, depth:, LANES:] = top


def split_weights(weights):
    count, depth, width = weights.shape
    return pl.pallas_call(
        weights_kernel,
        out_shape=jax.ShapeDtypeStruct((count, 2 * depth, 2 * width), jnp.bfloat16),
    )(weights)


def slots_kernel(slots_ref, weights_ref, kept_ref, *refs, targets):
    moved = len(targets)
    out_refs, (held_ref, sems) = refs[:moved], refs[moved:]
    peers = slots_ref.shape[0]
    blocks = slots_ref.shape[1]
    tops, mids = [], []
    for k in range(blocks):
        top, mid = split(slots_ref[:, k].reshape(peers * 8, LANES))
        tops.append(top)
        mids.append(mid)
    whole = jnp.concatenate(tops + mids, axis=1)

    def product(d):
        both = jnp.dot(whole, weights_ref[d], preferred_element_type=jnp.float32)
        return both[:, :LANES] + both[:, LANES:]

    copies = []
    for i, d in enumerate(targets):
        held_ref[i] = product(d)
        copies.append(pltpu.make_async_copy(held_ref.at[i], out_refs[i], sems.at[i]))
        copies[-1].start()
    kept_ref[...] = product(0)
    for copy in copies:
        copy.wait()


def project_slots(slots, weights, targets):
    peers = slots.shape[0]
    moved = len(targets)
    shape = jax.ShapeDtypeStruct((peers * 8, LANES), jnp.float32)
    vmem = pl.BlockSpec(memory_space=pltpu.VMEM)
    return pl.pallas_call(
        functools.partial(slots_kernel, targets=targets),
        in_specs=[vmem, vmem],
        out_specs=[vmem] + [pl.BlockSpec(memory_space=pltpu.HBM)] * moved,
        out_shape=[shape] * (moved + 1),
        scratch_shapes=[
            pltpu.VMEM((moved,) + shape.shape, jnp.float32),
            pltpu.SemaphoreType.DMA((moved,)),
        ],
        compiler_params=pltpu.CompilerParams(vmem_limit_bytes=12 * 2**20),
        cost_estimate=pl.CostEstimate(flops=10**7, bytes_accessed=4 * 2**20, transcendentals=0),
    )(slots, weights)


def scatter_kernel(rows_hbm, *refs, blocks, bases, last):
    *refs, rows_ref, rows_sem = refs
    lists = pltpu.make_async_copy(rows_hbm, rows_ref, rows_sem)
    lists.start()
    parts = refs[:blocks]
    base_refs = refs[blocks : blocks + bases]
    bias_ref = refs[blocks + bases] if last else None
    refs = refs[blocks + bases + last :]
    if last:
        out_hbm, *sums, out_ref, sems = refs
    else:
        out_ref, *sums = refs
    for total in sums:
        total[...] = jnp.zeros_like(total)
    lists.wait()
    left = left_half((1, LANES))
    zero = jnp.zeros((1, LANES), jnp.float32)
    lanes = len(sums) // 2
    for d, part in enumerate(parts):
        count = part.shape[0]

        def add(g, carry, part=part, d=d, count=count):
            for i in range(lanes):
                row = g * lanes + i
                value = part[pl.ds(row, 1), :]
                first = rows_ref[(d * count + row) * 2]
                second = rows_ref[(d * count + row) * 2 + 1]
                sums[2 * i][pl.ds(first, 1), :] += jnp.where(left, value, zero)
                sums[2 * i + 1][pl.ds(second, 1), :] += jnp.where(left, zero, value)
            return carry

        lax.fori_loop(0, count // lanes, add, 0, unroll=8)
    width = 512
    copies = []
    for c in range(out_ref.shape[1] // width):
        columns = slice(c * width, (c + 1) * width)
        whole = functools.reduce(lambda a, b: a + b, [total[columns, :] for total in sums])
        turned = whole.T
        result = turned[:HALF] + turned[HALF:]
        for base in base_refs:
            result = result + base[:, columns]
        out_ref[:, columns] = jnp.maximum(result + bias_ref[...], 0.0) if last else result
        if last:
            copies.append(pltpu.make_async_copy(out_ref.at[:, columns], out_hbm.at[:, columns], sems.at[c]))
            copies[-1].start()
    for copy in copies:
        copy.wait()


def scatter_rows(parts, rows, bases, row_count, bias=None):
    last = bias is not None
    vmem = pl.BlockSpec(memory_space=pltpu.VMEM)
    return pl.pallas_call(
        functools.partial(scatter_kernel, blocks=len(parts), bases=len(bases), last=last),
        in_specs=[pl.BlockSpec(memory_space=pltpu.HBM)] + [vmem] * (len(parts) + len(bases) + last),
        out_specs=pl.BlockSpec(memory_space=pltpu.HBM) if last else vmem,
        out_shape=jax.ShapeDtypeStruct((HALF, row_count), jnp.float32),
        scratch_shapes=[pltpu.VMEM((row_count + 8, LANES), jnp.float32)] * 4
        + ([pltpu.VMEM((HALF, row_count), jnp.float32), pltpu.SemaphoreType.DMA((8,))] if last else [])
        + [pltpu.SMEM(rows.shape, jnp.int32), pltpu.SemaphoreType.DMA],
        compiler_params=pltpu.CompilerParams(vmem_limit_bytes=13 * 2**20),
        cost_estimate=pl.CostEstimate(flops=10**7, bytes_accessed=16 * 2**20, transcendentals=0),
    )(rows, *parts, *bases, *([bias] if last else []))


def shifted(value, count, step):
    return lax.ppermute(value, "feat", [(i, (i + step) % count) for i in range(count)])


def per_device(
    features,
    w_self,
    w_neigh,
    out_bias,
    hub_rows,
    replica_send_rows,
    ret_rows,
    tile_src,
    tile_dst,
    tile_vals,
    *,
    feat,
):
    xt = features.T
    peers, slot = replica_send_rows.shape[1:]
    ret = ret_rows.shape[2]
    outgoing = gather_rows(xt, replica_send_rows[0], hub_rows[0])
    mirror = lax.all_to_all(outgoing, "dom", split_axis=0, concat_axis=0, tiled=True)

    me = lax.axis_index("feat")
    width = xt.shape[0]
    neighbours = [w_neigh] + [shifted(w_neigh, feat, -d) for d in range(1, feat)]
    xt, tiles, neighbours = lax.optimization_barrier((xt, tile_vals[0], neighbours))
    blocks = [xt] + [shifted(xt, feat, d) for d in range(1, feat)]
    split_vals, tile_order = split_tiles(tiles, tile_src[0], tile_dst[0])

    side = (lax.axis_index("dom") % 2).astype(jnp.int32).reshape(1)
    tile_order = jnp.concatenate([tile_order, jnp.zeros((31,), jnp.int32), side])
    mirror, split_vals, tile_order = lax.optimization_barrier((mirror, split_vals, tile_order))
    rows = slot // 2
    hub_count = hub_rows.shape[1] * peers // slot
    hub_half = mirror[:, rows:]
    hub_other = lax.ppermute(hub_half, "dom", [(i, i ^ 1) for i in range(peers)])
    partial, hub_vals = listed_tiles(split_vals, mirror, tile_order, rows, hub_count, peers * ret // slot)
    partial = hub_tiles(hub_vals, hub_half, hub_other, partial, tile_order)
    partial, blocks, neighbours, w_self, ret_rows = lax.optimization_barrier(
        (partial, blocks, neighbours, w_self, ret_rows)
    )
    slots = lax.all_to_all(partial, ("dom", "feat"), split_axis=0, concat_axis=0, tiled=True)

    self_rows = w_self.reshape(feat, width, -1)
    self_rows = jnp.concatenate(
        [lax.dynamic_index_in_dim(self_rows, (me - d) % feat, 0, False) for d in range(feat)]
    )
    own = lax.dot_general(
        self_rows,
        jnp.concatenate(blocks),
        (((0,), (0,)), ((), ())),
        precision=lax.Precision.HIGHEST,
        preferred_element_type=jnp.float32,
    )
    weights = []
    for mine in neighbours:
        mine = mine.reshape(feat, width, width)
        empty = jnp.zeros_like(mine)
        weights.append(
            jnp.stack([jnp.concatenate([mine, empty], 2), jnp.concatenate([empty, mine], 2)], 1).reshape(
                feat * LANES, LANES
            )
        )
    weights = split_weights(jnp.stack(weights))
    quarters = ret_rows[0].reshape(peers, feat, 2, 8).transpose(1, 0, 3, 2)
    order = [
        lax.dynamic_index_in_dim(quarters, (me - d) % feat, 0, False).reshape(-1) for d in range(feat)
    ]
    far = feat // 2
    near = [d for d in range(feat - 1, 0, -1) if d != far]
    near_rows = jnp.concatenate([order[d] for d in near])
    bias = out_bias[:, None]
    row_count = features.shape[0]
    slots, own, weights, near_rows, order, bias = lax.optimization_barrier(
        (slots, own, weights, near_rows, order, bias)
    )
    slots = slots.reshape(peers, feat, 8, LANES)
    targets = (far, *near)
    kept, *parts = project_slots(slots, weights, targets)
    moved = {d: shifted(part, feat, d) for d, part in zip(targets, parts)}
    total = scatter_rows([kept], order[0], [own], row_count)
    total = scatter_rows([moved[far]], order[far], [total], row_count)
    return scatter_rows([moved[d] for d in near], near_rows, [total], row_count, bias).T


def solution(mesh):
    return jax.shard_map(
        functools.partial(per_device, feat=mesh.shape["feat"]),
        mesh=mesh,
        in_specs=(
            P("dom", "feat"),
            P(None, "feat"),
            P(None, "feat"),
            P("feat"),
            P("dom", None),
            P("dom", None, None),
            P("dom", None, None),
            P("dom", None),
            P("dom", None),
            P("dom", None, None, None),
        ),
        out_specs=P("dom", "feat"),
        check_vma=False,
    )
```
